128 devices in a mesh: img: 8 (over y, core), orient: 16 (over x, z).
Axes of the slice: x: 4, y: 4, z: 4, core: 2. Of those that a mesh axis runs over, the one named last changes fastest.
Arguments:
- images: bfloat16 [4096, 16384], P(('img', 'orient')), may hold values from -8 to 8
- projections: bfloat16 [2048, 16384], P('orient'), may hold values from -0.2 to 0.2
- noise_weight: float32 [16384], replicated, may hold values from 0.5 to 2
- trans_offset: int32 [4096], P('img'), may hold values from 0 to 15
- search_list: int32 [128, 3], P('img'), may hold values from -1 to 15, as said below
Outputs:
- weighted_sum: float32 [2048, 16384], P('orient', 'img')
- log_norm: float32 [4096], P(('img', 'orient'))
The draws below stay inside these ranges and needn't reach their ends.
Inputs may be any that keep to these rules, and one draw needn't show every extreme that they name: `search_list`: row b holds one to 3 distinct block ids q with (q - b) mod 16 equal to 15, 0 or 1, in any order, and -1 in its other entries; some row holds 3 ids.
All inputs are finite; a program needn't handle non-finite values.
Results may differ from the reference program's by a relative error of at most 0.011.
Values may be sent and summed in bfloat16 or wider, within the bound.
A program may use at most 256 MiB of HBM per device.

```python
import math
import jax
import jax.numpy as jnp
from jax import lax

BOX = 128
F = 16384
PBS = 128
IMG_DEV = 32
NT = 8
BLOCKS = 128
IMAGES = 4096
PROJ = 2048
N_ORIENT = 16


def projection_values(base_key, pair_size):
    scale_key = jax.random.fold_in(base_key, 11)
    value_key = jax.random.fold_in(base_key, 12)
    scales = jnp.exp(jax.random.uniform(scale_key, (PROJ // pair_size,), jnp.float32, math.log(0.5), math.log(2.0)))
    scales = jnp.repeat(scales, pair_size)
    normal_part = jax.random.truncated_normal(value_key, -6.0, 6.0, (PROJ, F), jnp.float32)
    values = normal_part
    return 0.015625 * scales[:, None] * values


def offset_values(base_key):
    return jax.random.randint(jax.random.fold_in(base_key, 21), (IMAGES,), 0, 16, jnp.int32)


def list_values(base_key):
    flag_key = jax.random.fold_in(base_key, 31)
    full_key = jax.random.fold_in(base_key, 32)
    roll_key = jax.random.fold_in(base_key, 33)
    flags = jax.random.randint(flag_key, (BLOCKS, 3), 0, 5, jnp.int32) < 3
    empty_rows = jnp.logical_not(jnp.any(flags, axis=1))
    centre = jnp.arange(3, dtype=jnp.int32)[None, :] == 1
    flags = flags | empty_rows[:, None] & centre
    full_row = jax.random.randint(full_key, (), 0, BLOCKS, jnp.int32)
    flags = flags | (jnp.arange(BLOCKS, dtype=jnp.int32)[:, None] == full_row)
    rolls = jax.random.randint(roll_key, (BLOCKS, 1), 0, 3, jnp.int32)
    positions = (jnp.arange(3, dtype=jnp.int32)[None, :] + rolls) % 3
    chosen = jnp.take_along_axis(flags, positions, axis=1)
    owners = jnp.arange(BLOCKS, dtype=jnp.int32)[:, None] % N_ORIENT
    entries = (owners + positions - 1) % N_ORIENT
    return jnp.where(chosen, entries, -1).astype(jnp.int32)


def draw_search_list(key, part):
    return list_values(key)


def draw_trans_offset(key, part):
    return offset_values(key)


def draw_projections(key, part):
    values = projection_values(key, 1)
    return values.astype(jnp.bfloat16)


def draw_images(key, part):
    own_key = jax.random.fold_in(key, 5)
    values = jax.random.truncated_normal(jax.random.fold_in(own_key, 4), -8.0, 8.0, (IMAGES, F), jnp.float32)
    return values.astype(jnp.bfloat16)


def setup_inputs(seed: int = 0) -> dict:
    streams_of = jax.random.split(jax.random.key(seed), 6)
    images = draw_images(jax.random.fold_in(streams_of[5], 71), 0)
    projections = draw_projections(jax.random.fold_in(streams_of[5], 71), 0)
    noise_weight = jnp.clip(jnp.exp(jax.random.uniform(streams_of[2], (F,), jnp.float32, math.log(0.5), math.log(2.0))), 0.5, 2.0)
    trans_offset = draw_trans_offset(jax.random.fold_in(streams_of[5], 71), 0)
    search_list = draw_search_list(jax.random.fold_in(streams_of[5], 71), 0)
    return {"images": images, "projections": projections, "noise_weight": noise_weight, "trans_offset": trans_offset, "search_list": search_list}


mask_floor = -1.0e30


def align_images(block_images, block_offsets):
    half_box = BOX // 2
    plane_size = BOX * half_box
    count = block_images.shape[0]
    freq_index = jnp.arange(BOX, dtype=jnp.int32)
    freq_x = jnp.where(freq_index < half_box, freq_index, freq_index - BOX)
    freq_y = jnp.arange(half_box, dtype=jnp.int32)
    shift_steps = jnp.arange(NT, dtype=jnp.int32)
    shift_x = block_offsets[:, None] % 4 - 2 + shift_steps[None, :] % 4
    shift_y = block_offsets[:, None] // 4 - 2 + shift_steps[None, :] // 4
    turns_x = (shift_x[:, :, None] * freq_x[None, None, :]) % BOX
    turns_y = (shift_y[:, :, None] * freq_y[None, None, :]) % BOX
    angle_x = turns_x.astype(jnp.float32) * (2.0 * math.pi / BOX)
    angle_y = turns_y.astype(jnp.float32) * (2.0 * math.pi / BOX)
    cos_x = jnp.cos(angle_x)[:, :, :, None]
    sin_x = jnp.sin(angle_x)[:, :, :, None]
    cos_y = jnp.cos(angle_y)[:, :, None, :]
    sin_y = jnp.sin(angle_y)[:, :, None, :]
    cosine = (cos_x * cos_y - sin_x * sin_y).reshape(count, NT, plane_size)
    sine_part = (sin_x * cos_y + cos_x * sin_y).reshape(count, NT, plane_size)
    real_part = block_images[:, None, :plane_size].astype(jnp.float32)
    imag_part = block_images[:, None, plane_size:].astype(jnp.float32)
    moved = jnp.concatenate([real_part * cosine + imag_part * sine_part, imag_part * cosine - real_part * sine_part], axis=2)
    return moved.astype(jnp.bfloat16)


def reference(images, projections, noise_weight, trans_offset, search_list):
    running_sum = jnp.zeros((PROJ, F), jnp.float32)

    def visit(running_sum, block_index):
        orient_place = block_index % N_ORIENT
        candidates = ((orient_place - 1 + jnp.arange(3, dtype=jnp.int32)) % N_ORIENT).astype(jnp.int32)
        proj_rim = jnp.concatenate([lax.dynamic_slice_in_dim(projections, candidates[slot] * PBS, PBS, 0) for slot in range(3)], axis=0)
        block_images = lax.dynamic_slice_in_dim(images, block_index * IMG_DEV, IMG_DEV, 0)
        block_offsets = lax.dynamic_slice_in_dim(trans_offset, block_index * IMG_DEV, IMG_DEV, 0)
        list_row = lax.dynamic_index_in_dim(search_list, block_index, 0, keepdims=False)
        listed = jnp.any(list_row[None, :] == candidates[:, None], axis=1)
        col_mask = jnp.repeat(listed, PBS)
        aligned_rows = align_images(block_images, block_offsets).reshape(IMG_DEV * NT, F)
        weighted = (proj_rim.astype(jnp.float32) * noise_weight[None, :]).astype(jnp.bfloat16)
        proj_power = jnp.sum(noise_weight[None, :] * jnp.square(proj_rim.astype(jnp.float32)), axis=1)
        scores = jnp.dot(aligned_rows, weighted.T, preferred_element_type=jnp.float32) - 0.5 * proj_power[None, :]
        scores = scores.reshape(IMG_DEV, NT, 3 * PBS)
        scores = jnp.where(col_mask[None, None, :], scores, mask_floor)
        row_max = jnp.max(scores, axis=(1, 2), keepdims=True)
        norms = row_max[:, 0, 0] + jnp.log(jnp.sum(jnp.exp(scores - row_max), axis=(1, 2)))
        posterior = jnp.exp(scores - norms[:, None, None]).astype(jnp.bfloat16).reshape(IMG_DEV * NT, 3 * PBS)
        block_sums = jnp.dot(posterior.T, aligned_rows, preferred_element_type=jnp.float32)
        for slot in range(3):
            start = candidates[slot] * PBS
            current = lax.dynamic_slice_in_dim(running_sum, start, PBS, 0)
            running_sum = lax.dynamic_update_slice_in_dim(running_sum, current + block_sums[slot * PBS:(slot + 1) * PBS], start, 0)
        return running_sum, norms

    running_sum, all_norms = lax.scan(visit, running_sum, jnp.arange(BLOCKS, dtype=jnp.int32))
    return running_sum, all_norms.reshape(IMAGES)
```

```python
import functools
import math

import jax
import jax.numpy as jnp
import numpy as np
from jax import lax
from jax.experimental import pallas as pl
from jax.experimental.pallas import tpu as pltpu
from jax.sharding import PartitionSpec as P

BOX = 128
HALF = BOX * BOX // 2
NT = 8
N_OFF = 16
MESH = pl.DeviceIdType.MESH
FLOOR = -1e30

CH = 1024
NCH = HALF // CH
PIECE = 256
HS = 1024
SUB = 256
F32 = jnp.float32
BF16 = jnp.bfloat16


def phase_tables():
    steps = np.arange(BOX)
    unit = 2.0 * math.pi / BOX
    cos1, sin1 = np.cos(steps * unit), np.sin(steps * unit)
    t, s, f = np.arange(N_OFF)[:, None, None], np.arange(NT)[None, :, None], np.arange(HALF)[None, None, :]
    kx, ky = f // (BOX // 2), f % (BOX // 2)
    fx = np.where(kx < BOX // 2, kx, kx - BOX)
    turn_x = (fx * (t % 4 - 2 + s % 4)) % BOX
    turn_y = (ky * (t // 4 - 2 + s // 4)) % BOX
    cx, sx, cy, sy = cos1[turn_x], sin1[turn_x], cos1[turn_y], sin1[turn_y]
    return np.stack([cx * cy - sx * sy, sx * cy + cx * sy], axis=1).astype(np.float32)


def kernel(
    img_hbm, proj_hbm, tab_hbm, w_hbm, off, listed,
    out_ref, norm_ref,
    al, halo, own, wp, tab, w, score, power, lse, lse1, lse2, post, csend, crecv, ysend, yrecv,
    img_send, img_recv, loc_sem, tab_sem, proj_sem, lse_send, lse_recv, c_send, c_recv, y_send, y_recv,
):
    rows = img_hbm.shape[0]
    nrow = rows * NT
    n_img, n_or = lax.axis_size("img"), lax.axis_size("orient")
    i, o = lax.axis_index("img"), lax.axis_index("orient")
    core = lax.rem(i, 2)
    chip = lax.div(i, 2)
    n_y = n_img // 2
    before, after = lax.rem(o + n_or - 1, n_or), lax.rem(o + 1, n_or)
    before2, after2 = lax.rem(o + n_or - 2, n_or), lax.rem(o + 2, n_or)
    mate = (i + 1 - 2 * core, o)
    up = (lax.rem(i + 2, n_img), o)
    down = (lax.rem(i + n_img - 2, n_img), o)

    def remote(src, dst, ssem, rsem, dev):
        return pltpu.make_async_remote_copy(
            src_ref=src, dst_ref=dst, send_sem=ssem, recv_sem=rsem, device_id=dev, device_id_type=MESH
        )

    own_copy = pltpu.make_async_copy(img_hbm, own, loc_sem.at[0])
    own_copy.start()
    w_copy = pltpu.make_async_copy(w_hbm, w, loc_sem.at[1])
    w_copy.start()

    def coef(k, size=CH):
        return pl.ds(pl.multiple_of(k * size, size), size)

    def imag(k, size=CH):
        return pl.ds(pl.multiple_of(HALF + k * size, size), size)

    def tab_copy(k):
        return pltpu.make_async_copy(tab_hbm.at[:, :, :, coef(k)], tab.at[:, :, :, coef(k)], tab_sem.at[k])

    def proj_copy(k, part):
        cols = coef(k) if part == 0 else imag(k)
        return pltpu.make_async_copy(proj_hbm.at[:, cols], wp.at[:, cols], proj_sem.at[part, k])

    def start_local(k, carry):
        tab_copy(k).start()
        proj_copy(k, 0).start()
        proj_copy(k, 1).start()
        return carry

    lax.fori_loop(0, NCH, start_local, 0)

    barrier = pltpu.get_barrier_semaphore()
    partners = [(i, before), (i, after), (i, before2), (i, after2), mate, up, down]
    for dev in partners:
        pl.semaphore_signal(barrier, inc=1, device_id=dev, device_id_type=MESH)
    pl.semaphore_wait(barrier, len(partners))

    def img_copy(side, k, part):
        cols = coef(k) if part == 0 else imag(k)
        dev = (i, after) if side == 0 else (i, before)
        return remote(
            img_hbm.at[:, cols], halo.at[side, :, cols], img_send.at[side, part, k], img_recv.at[side, part, k], dev
        )

    def start_images(k, carry):
        for part in range(2):
            for side in range(2):
                img_copy(side, k, part).start()
        return carry

    lax.fori_loop(0, NCH, start_images, 0)

    def weigh(k):
        def step(p, acc):
            cols = pl.ds(pl.multiple_of(k * CH + p * PIECE, PIECE), PIECE)
            cols2 = pl.ds(pl.multiple_of(HALF + k * CH + p * PIECE, PIECE), PIECE)
            for c in (cols, cols2):
                x = wp[:, c].astype(F32)
                y = x * w[:, c]
                wp[:, c] = y.astype(BF16)
                q = x * y
                for j in range(PIECE // 128):
                    acc = acc + q[:, j * 128:(j + 1) * 128]
            return acc

        power[...] += lax.fori_loop(0, CH // PIECE, step, jnp.zeros(power.shape, F32))

    def align(src, block, slot, k):
        def step(it, carry):
            g, p = lax.div(it, CH // PIECE), lax.rem(it, CH // PIECE)
            cols = pl.ds(pl.multiple_of(k * CH + p * PIECE, PIECE), PIECE)
            cols2 = pl.ds(pl.multiple_of(HALF + k * CH + p * PIECE, PIECE), PIECE)
            r16 = pl.ds(pl.multiple_of(g * 16, 16), 16)
            re = src[r16, cols].astype(F32)
            im = src[r16, cols2].astype(F32)
            for pair in range(8):
                res, ims = [], []
                for h in range(2):
                    n = 2 * pair + h
                    t = off[block * rows + g * 16 + n]
                    c = tab[t, 0, :, cols]
                    d = tab[t, 1, :, cols]
                    rb = jnp.broadcast_to(re[n:n + 1, :], (NT, PIECE))
                    ib = jnp.broadcast_to(im[n:n + 1, :], (NT, PIECE))
                    res.append(rb * c + ib * d)
                    ims.append(ib * c - rb * d)
                dst = pl.ds(pl.multiple_of(slot * nrow + g * 128 + pair * 16, 16), 16)
                al[dst, cols] = jnp.concatenate(res, axis=0).astype(BF16)
                al[dst, cols2] = jnp.concatenate(ims, axis=0).astype(BF16)
            return carry

        lax.fori_loop(0, (rows // 16) * (CH // PIECE), step, 0)

    def add_scores(slot, k):
        here = pl.ds(slot * nrow, nrow)
        total = score[here, :]
        for cols in (coef(k), imag(k)):
            total += lax.dot_general(
                al[here, cols], wp[:, cols], (((1,), (1,)), ((), ())), preferred_element_type=F32
            )
        score[here, :] = total

    score[...] = jnp.zeros(score.shape, F32)
    power[...] = jnp.zeros(power.shape, F32)
    own_copy.wait()
    w_copy.wait()

    def wait_tables(k, carry):
        tab_copy(k).wait()
        return carry

    lax.fori_loop(0, NCH, wait_tables, 0)

    def own_chunk(k, carry):
        proj_copy(k, 0).wait()
        proj_copy(k, 1).wait()
        weigh(k)
        align(own, o, 0, k)
        add_scores(0, k)
        return carry

    lax.fori_loop(0, NCH, own_chunk, 0)

    half_power = 0.5 * jnp.sum(power[...].T, axis=0, keepdims=True)

    def finish_scores(slot, block):
        hit = (listed[block, 0] == o) | (listed[block, 1] == o) | (listed[block, 2] == o)
        keep = jnp.where(hit, 1.0, 0.0)
        floor = jnp.where(hit, 0.0, FLOOR)
        here = pl.ds(slot * nrow, nrow)
        x = (score[here, :] - half_power) * keep + floor
        score[here, :] = x
        x3 = x.reshape(rows, NT, 128)
        m = jnp.max(jnp.max(x3, axis=1), axis=1, keepdims=True)
        mb = jnp.broadcast_to(m, (rows, 128))
        e = jnp.exp(x3 - mb[:, None, :])
        total = jnp.sum(jnp.sum(e, axis=1), axis=1, keepdims=True)
        return jnp.broadcast_to(m + jnp.log(total), (rows, 128))

    lse[1] = finish_scores(0, o)

    def halo_chunk(k, carry):
        for side, block in ((0, before), (1, after)):
            for part in range(2):
                img_copy(side, k, part).wait_recv()
            align(halo.at[side], block, 1 + side, k)
            add_scores(1 + side, k)
        return carry

    lax.fori_loop(0, NCH, halo_chunk, 0)

    lse[2] = finish_scores(1, before)
    lse[0] = finish_scores(2, after)

    to_after = remote(lse.at[pl.ds(0, 2)], lse1.at[0], lse_send.at[0], lse_recv.at[0], (i, after))
    to_before = remote(lse.at[pl.ds(1, 2)], lse1.at[1], lse_send.at[1], lse_recv.at[1], (i, before))
    to_after2 = remote(lse.at[0], lse2.at[0], lse_send.at[2], lse_recv.at[2], (i, after2))
    to_before2 = remote(lse.at[2], lse2.at[1], lse_send.at[3], lse_recv.at[3], (i, before2))
    lse_copies = [to_after2, to_before2, to_after, to_before]
    for copy in lse_copies:
        copy.start()
    for copy in lse_copies:
        copy.wait_recv()

    def combine(a, b, c):
        m = jnp.maximum(jnp.maximum(a, b), c)
        return m + jnp.log(jnp.exp(a - m) + jnp.exp(b - m) + jnp.exp(c - m))

    norms = [
        combine(lse[1], lse1[0, 0], lse1[1, 1]),
        combine(lse[2], lse1[0, 1], lse2[0]),
        combine(lse[0], lse1[1, 0], lse2[1]),
    ]
    norm_ref[...] = norms[0].T[0:1, :]
    for slot in range(3):
        x3 = score[pl.ds(slot * nrow, nrow), :].reshape(rows, NT, 128)
        p = jnp.exp(x3 - norms[slot][:, None, :]).reshape(nrow, 128)
        post[:, pl.ds(slot * nrow, nrow)] = p.T.astype(BF16)

    chip_up, chip_down = lax.rem(chip + 1, n_y), lax.rem(chip + n_y - 1, n_y)
    chip_far = lax.rem(chip + 2, n_y)
    plan = [
        (chip_far, 0, None, 0, 0),
        (chip_far, 1, None, 1, 3),
        (chip_up, 1, None, 0, 1),
        (chip_down, 0, None, 1, 4),
        (chip_up, 0, 0, 0, 2),
        (chip_down, 1, 3, 1, 5),
        (chip, 0, None, None, None),
        (chip, 1, None, None, None),
    ]

    def sums(dest, parity, half, j):
        start = (dest * 2 + parity) * (2 * HS) + half * HS + j * SUB
        return jnp.dot(
            post[...], al[:, pl.ds(pl.multiple_of(start, SUB), SUB)], preferred_element_type=F32
        )

    def core_copy(q):
        return remote(csend.at[q], crecv.at[q], c_send.at[q], c_recv.at[q], mate)

    def y_copy(slot, way):
        dev = up if way == 0 else down
        return remote(ysend.at[slot], yrecv.at[slot], y_send.at[slot], y_recv.at[slot], dev)

    def for_mate(q):
        dest, half = plan[q][0], plan[q][1]

        def step(j, carry):
            csend[q, :, pl.ds(pl.multiple_of(j * SUB, SUB), SUB)] = sums(dest, 1 - core, half, j).astype(BF16)
            return carry

        lax.fori_loop(0, HS // SUB, step, 0)
        core_copy(q).start()

    for_mate(0)
    for q, (dest, half, add, way, slot) in enumerate(plan):
        if q + 1 < len(plan):
            for_mate(q + 1)
        core_copy(q).wait_recv()
        if add is not None:
            y_copy(add, 0 if add < 3 else 1).wait_recv()

        def step(j, carry):
            cols = pl.ds(pl.multiple_of(j * SUB, SUB), SUB)
            total = sums(dest, core, half, j) + crecv[q, :, cols].astype(F32)
            if add is not None:
                total = total + yrecv[add, :, cols].astype(F32)
            if slot is not None:
                ysend[slot, :, cols] = total.astype(BF16)
            else:
                out_ref[:, pl.ds(pl.multiple_of(half * HS + j * SUB, SUB), SUB)] = total
            return carry

        lax.fori_loop(0, HS // SUB, step, 0)
        if slot is not None:
            y_copy(slot, way).start()

    for pair, half in (((4, 2), 0), ((1, 5), 1)):
        for slot in pair:
            y_copy(slot, 0 if slot < 3 else 1).wait_recv()

        def step(j, carry):
            cols = pl.ds(pl.multiple_of(j * SUB, SUB), SUB)
            out_cols = pl.ds(pl.multiple_of(half * HS + j * SUB, SUB), SUB)
            out_ref[:, out_cols] += yrecv[pair[0], :, cols].astype(F32) + yrecv[pair[1], :, cols].astype(F32)
            return carry

        lax.fori_loop(0, HS // SUB, step, 0)

    def finish_images(k, carry):
        for part in range(2):
            for side in range(2):
                img_copy(side, k, part).wait_send()
        return carry

    lax.fori_loop(0, NCH, finish_images, 0)
    for copy in lse_copies:
        copy.wait_send()
    for q in range(len(plan)):
        core_copy(q).wait_send()
    for slot in range(6):
        y_copy(slot, 0 if slot < 3 else 1).wait_send()


def per_device(images, projections, noise_weight, trans_offset, search_list):
    rows, width = images.shape
    block = projections.shape[0]
    n_img = lax.axis_size("img")
    nrow = rows * NT
    any_space = pl.BlockSpec(memory_space=pl.ANY)
    smem = pl.BlockSpec(memory_space=pltpu.SMEM)
    vmem = pl.BlockSpec(memory_space=pltpu.VMEM)
    dma = pltpu.SemaphoreType.DMA
    weighted_sum, log_norm = pl.pallas_call(
        kernel,
        out_shape=(
            jax.ShapeDtypeStruct((block, width // n_img), F32),
            jax.ShapeDtypeStruct((1, rows), F32),
        ),
        in_specs=[any_space, any_space, any_space, any_space, smem, smem],
        out_specs=(vmem, vmem),
        scratch_shapes=[
            pltpu.VMEM((3 * nrow, width), BF16),
            pltpu.VMEM((2, rows, width), BF16),
            pltpu.VMEM((rows, width), BF16),
            pltpu.VMEM((block, width), BF16),
            pltpu.VMEM((N_OFF, 2, NT, HALF), F32),
            pltpu.VMEM((1, width), F32),
            pltpu.VMEM((3 * nrow, block), F32),
            pltpu.VMEM((block, 128), F32),
            pltpu.VMEM((3, rows, 128), F32),
            pltpu.VMEM((2, 2, rows, 128), F32),
            pltpu.VMEM((2, rows, 128), F32),
            pltpu.VMEM((block, 3 * nrow), BF16),
            pltpu.VMEM((8, block, HS), BF16),
            pltpu.VMEM((8, block, HS), BF16),
            pltpu.VMEM((6, block, HS), BF16),
            pltpu.VMEM((6, block, HS), BF16),
            dma((2, 2, NCH)), dma((2, 2, NCH)),
            dma((2,)), dma((NCH,)), dma((2, NCH)),
            dma((4,)), dma((4,)),
            dma((8,)), dma((8,)),
            dma((6,)), dma((6,)),
        ],
        compiler_params=pltpu.CompilerParams(
            collective_id=0, has_side_effects=True, vmem_limit_bytes=60 * 1024 * 1024
        ),
    )(images, projections, jnp.asarray(phase_tables()), noise_weight.reshape(1, width), trans_offset, search_list)
    return weighted_sum, log_norm.reshape(rows)


def solution(mesh):
    in_specs = (P(("img", "orient"), None), P("orient", None), P(), P("img"), P("img", None))
    out_specs = (P("orient", "img"), P(("img", "orient")))
    return jax.shard_map(
        per_device, mesh=mesh, in_specs=in_specs, out_specs=out_specs, check_vma=False
    )
```

```python
import functools
import math

import jax
import jax.numpy as jnp
import numpy as np
from jax import lax
from jax.experimental import pallas as pl
from jax.experimental.pallas import tpu as pltpu
from jax.sharding import PartitionSpec as P

BOX = 128
HALF = BOX * BOX // 2
NT = 8
N_OFF = 16
MESH = pl.DeviceIdType.MESH
FLOOR = -1e30

CH = 1024
NCH = HALF // CH
PIECE = 512
HS = 1024
SUB = 1024
F32 = jnp.float32
BF16 = jnp.bfloat16


def phase_tables():
    steps = np.arange(BOX)
    unit = 2.0 * math.pi / BOX
    cos1, sin1 = np.cos(steps * unit), np.sin(steps * unit)
    t, s, f = np.arange(N_OFF)[:, None, None], np.arange(NT)[None, :, None], np.arange(HALF)[None, None, :]
    kx, ky = f // (BOX // 2), f % (BOX // 2)
    fx = np.where(kx < BOX // 2, kx, kx - BOX)
    turn_x = (fx * (t % 4 - 2 + s % 4)) % BOX
    turn_y = (ky * (t // 4 - 2 + s // 4)) % BOX
    cx, sx, cy, sy = cos1[turn_x], sin1[turn_x], cos1[turn_y], sin1[turn_y]
    return np.stack([cx * cy - sx * sy, sx * cy + cx * sy], axis=1).astype(np.float32)


def kernel(
    img_hbm, proj_hbm, tab_hbm, w_hbm, off, listed,
    out_ref, norm_ref,
    al, halo, own, wp, tab, w, score, power, lse, others, post, csend, crecv, ysend, yrecv, stage,
    img_send, img_recv, loc_sem, tab_sem, proj_sem, lse_send, lse_recv, c_send, c_recv, y_send, y_recv,
):
    rows = img_hbm.shape[0]
    nrow = rows * NT
    n_img, n_or = lax.axis_size("img"), lax.axis_size("orient")
    i, o = lax.axis_index("img"), lax.axis_index("orient")
    core = lax.rem(i, 2)
    chip = lax.div(i, 2)
    n_y = n_img // 2
    before, after = lax.rem(o + n_or - 1, n_or), lax.rem(o + 1, n_or)
    before2, after2 = lax.rem(o + n_or - 2, n_or), lax.rem(o + 2, n_or)
    mate = (i + 1 - 2 * core, o)
    up = (lax.rem(i + 2, n_img), o)
    down = (lax.rem(i + n_img - 2, n_img), o)

    def remote(src, dst, ssem, rsem, dev):
        return pltpu.make_async_remote_copy(
            src_ref=src, dst_ref=dst, send_sem=ssem, recv_sem=rsem, device_id=dev, device_id_type=MESH
        )

    own_copy = pltpu.make_async_copy(img_hbm, own, loc_sem.at[0])
    own_copy.start()
    w_copy = pltpu.make_async_copy(w_hbm, w, loc_sem.at[1])
    w_copy.start()

    def coef(k, size=CH):
        return pl.ds(pl.multiple_of(k * size, size), size)

    def imag(k, size=CH):
        return pl.ds(pl.multiple_of(HALF + k * size, size), size)

    def tab_copy(k):
        return pltpu.make_async_copy(tab_hbm.at[:, :, :, coef(k)], tab.at[:, :, :, coef(k)], tab_sem.at[k])

    def proj_copy(k, part):
        cols = coef(k) if part == 0 else imag(k)
        return pltpu.make_async_copy(proj_hbm.at[:, cols], wp.at[:, cols], proj_sem.at[part, k])

    def start_local(k, carry):
        tab_copy(k).start()
        proj_copy(k, 0).start()
        proj_copy(k, 1).start()
        return carry

    lax.fori_loop(0, NCH, start_local, 0)

    barrier = pltpu.get_barrier_semaphore()
    partners = [(i, before), (i, after), (i, before2), (i, after2), mate, up, down]
    for dev in partners:
        pl.semaphore_signal(barrier, inc=1, device_id=dev, device_id_type=MESH)
    pl.semaphore_wait(barrier, len(partners))

    def img_copy(side, k, part):
        cols = coef(k) if part == 0 else imag(k)
        dev = (i, after) if side == 0 else (i, before)
        return remote(
            img_hbm.at[:, cols], halo.at[side, :, cols], img_send.at[side, part, k], img_recv.at[side, part, k], dev
        )

    def start_images(k, carry):
        for part in range(2):
            for side in range(2):
                img_copy(side, k, part).start()
        return carry

    lax.fori_loop(0, NCH, start_images, 0)

    def weigh(k):
        def step(p, acc):
            cols = pl.ds(pl.multiple_of(k * CH + p * PIECE, PIECE), PIECE)
            cols2 = pl.ds(pl.multiple_of(HALF + k * CH + p * PIECE, PIECE), PIECE)
            for c in (cols, cols2):
                x = wp[:, c].astype(F32)
                y = x * w[:, c]
                wp[:, c] = y.astype(BF16)
                q = x * y
                for j in range(PIECE // 128):
                    acc = acc + q[:, j * 128:(j + 1) * 128]
            return acc

        power[...] += lax.fori_loop(0, CH // PIECE, step, jnp.zeros(power.shape, F32))

    def align(src, block, slot, k):
        def step(it, carry):
            g, p = lax.div(it, CH // PIECE), lax.rem(it, CH // PIECE)
            cols = pl.ds(pl.multiple_of(k * CH + p * PIECE, PIECE), PIECE)
            cols2 = pl.ds(pl.multiple_of(HALF + k * CH + p * PIECE, PIECE), PIECE)
            r16 = pl.ds(pl.multiple_of(g * 16, 16), 16)
            stage[0] = src[r16, cols].astype(F32)
            stage[1] = src[r16, cols2].astype(F32)
            for pair in range(8):
                res, ims = [], []
                for h in range(2):
                    n = 2 * pair + h
                    t = off[block * rows + g * 16 + n]
                    c = tab[t, 0, :, cols]
                    d = tab[t, 1, :, cols]
                    rb = stage[0, pl.ds(n, NT, stride=0), :]
                    ib = stage[1, pl.ds(n, NT, stride=0), :]
                    res.append(rb * c + ib * d)
                    ims.append(ib * c - rb * d)
                dst = pl.ds(pl.multiple_of(slot * nrow + g * 128 + pair * 16, 16), 16)
                al[dst, cols] = jnp.concatenate(res, axis=0).astype(BF16)
                al[dst, cols2] = jnp.concatenate(ims, axis=0).astype(BF16)
            return carry

        lax.fori_loop(0, (rows // 16) * (CH // PIECE), step, 0)

    def add_scores(slot, count, k):
        here = pl.ds(slot * nrow, count * nrow)
        total = score[here, :]
        for cols in (coef(k), imag(k)):
            total += lax.dot_general(
                al[here, cols], wp[:, cols], (((1,), (1,)), ((), ())), preferred_element_type=F32
            )
        score[here, :] = total

    lse[...] = jnp.zeros(lse.shape, F32)
    score[...] = jnp.zeros(score.shape, F32)
    power[...] = jnp.zeros(power.shape, F32)
    own_copy.wait()
    w_copy.wait()

    def wait_tables(k, carry):
        tab_copy(k).wait()
        return carry

    lax.fori_loop(0, NCH, wait_tables, 0)

    def own_chunk(k, carry):
        proj_copy(k, 0).wait()
        proj_copy(k, 1).wait()
        weigh(k)
        align(own, o, 0, k)
        add_scores(0, 1, k)
        return carry

    lax.fori_loop(0, NCH, own_chunk, 0)

    half_power = 0.5 * jnp.sum(power[...].T, axis=0, keepdims=True)

    diagonal = lax.broadcasted_iota(jnp.int32, (rows, 128), 0) == lax.broadcasted_iota(jnp.int32, (rows, 128), 1)

    def finish_scores(slot, block):
        hit = (listed[0, block] == o) | (listed[1, block] == o) | (listed[2, block] == o)
        keep = jnp.where(hit, 1.0, 0.0)
        floor = jnp.where(hit, 0.0, FLOOR)
        here = pl.ds(slot * nrow, nrow)
        x = (score[here, :] - half_power) * keep + floor
        score[here, :] = x
        x3 = x.reshape(rows, NT, 128)
        m = jnp.max(jnp.max(x3, axis=1), axis=1, keepdims=True)
        mb = jnp.broadcast_to(m, (rows, 128))
        e = jnp.exp(x3 - mb[:, None, :])
        total = jnp.sum(jnp.sum(e, axis=1), axis=1, keepdims=True)
        value = jnp.broadcast_to(m + jnp.log(total), (rows, 128))
        return jnp.sum(jnp.where(diagonal, value, 0.0), axis=0, keepdims=True)

    lse[1:2, :] = finish_scores(0, o)

    def halo_chunk(k, carry):
        for side, block in ((0, before), (1, after)):
            for part in range(2):
                img_copy(side, k, part).wait_recv()
            align(halo.at[side], block, 1 + side, k)
        add_scores(1, 2, k)
        return carry

    lax.fori_loop(0, NCH, halo_chunk, 0)

    lse[2:3, :] = finish_scores(1, before)
    lse[0:1, :] = finish_scores(2, after)

    lse_copies = [
        remote(lse, others.at[n], lse_send.at[n], lse_recv.at[n], (i, dev))
        for n, dev in enumerate((after2, before2, after, before))
    ]
    for copy in lse_copies:
        copy.start()
    for copy in lse_copies:
        copy.wait_recv()

    def combine(a, b, c):
        m = jnp.maximum(jnp.maximum(a, b), c)
        return m + jnp.log(jnp.exp(a - m) + jnp.exp(b - m) + jnp.exp(c - m))

    norms = [
        combine(lse[1:2, :], others[2, 0:1, :], others[3, 2:3, :]),
        combine(lse[2:3, :], others[2, 1:2, :], others[0, 0:1, :]),
        combine(lse[0:1, :], others[3, 1:2, :], others[1, 2:3, :]),
    ]
    norm_ref[...] = norms[0][:, :rows]
    for slot in range(3):
        x3 = score[pl.ds(slot * nrow, nrow), :].reshape(rows, NT, 128)
        each = jnp.sum(jnp.where(diagonal, jnp.broadcast_to(norms[slot], (rows, 128)), 0.0), axis=1, keepdims=True)
        p = jnp.exp(x3 - jnp.broadcast_to(each, (rows, 128))[:, None, :]).reshape(nrow, 128)
        post[:, pl.ds(slot * nrow, nrow)] = p.T.astype(BF16)

    chip_up, chip_down = lax.rem(chip + 1, n_y), lax.rem(chip + n_y - 1, n_y)
    chip_far = lax.rem(chip + 2, n_y)
    plan = [
        (chip_far, 0, None, 0, 0),
        (chip_far, 1, None, 1, 3),
        (chip_up, 1, None, 0, 1),
        (chip_down, 0, None, 1, 4),
        (chip_up, 0, 0, 0, 2),
        (chip_down, 1, 3, 1, 5),
        (chip, 0, None, None, None),
        (chip, 1, None, None, None),
    ]

    def sums(dest, parity, half, j):
        start = (dest * 2 + parity) * (2 * HS) + half * HS + j * SUB
        return jnp.dot(
            post[...], al[:, pl.ds(pl.multiple_of(start, SUB), SUB)], preferred_element_type=F32
        )

    def core_copy(q):
        return remote(csend.at[q], crecv.at[q], c_send.at[q], c_recv.at[q], mate)

    def y_copy(slot, way):
        dev = up if way == 0 else down
        return remote(ysend.at[slot], yrecv.at[slot], y_send.at[slot], y_recv.at[slot], dev)

    def for_mate(q):
        dest, half = plan[q][0], plan[q][1]

        def step(j, carry):
            csend[q, :, pl.ds(pl.multiple_of(j * SUB, SUB), SUB)] = sums(dest, 1 - core, half, j).astype(BF16)
            return carry

        lax.fori_loop(0, HS // SUB, step, 0)
        core_copy(q).start()

    for_mate(0)
    for q, (dest, half, add, way, slot) in enumerate(plan):
        if q + 1 < len(plan):
            for_mate(q + 1)
        core_copy(q).wait_recv()
        if add is not None:
            y_copy(add, 0 if add < 3 else 1).wait_recv()

        def step(j, carry):
            cols = pl.ds(pl.multiple_of(j * SUB, SUB), SUB)
            total = sums(dest, core, half, j) + crecv[q, :, cols].astype(F32)
            if add is not None:
                total = total + yrecv[add, :, cols].astype(F32)
            if slot is not None:
                ysend[slot, :, cols] = total.astype(BF16)
            else:
                out_ref[:, pl.ds(pl.multiple_of(half * HS + j * SUB, SUB), SUB)] = total
            return carry

        lax.fori_loop(0, HS // SUB, step, 0)
        if slot is not None:
            y_copy(slot, way).start()

    for pair, half in (((4, 2), 0), ((1, 5), 1)):
        for slot in pair:
            y_copy(slot, 0 if slot < 3 else 1).wait_recv()

        def step(j, carry):
            cols = pl.ds(pl.multiple_of(j * SUB, SUB), SUB)
            out_cols = pl.ds(pl.multiple_of(half * HS + j * SUB, SUB), SUB)
            out_ref[:, out_cols] += yrecv[pair[0], :, cols].astype(F32) + yrecv[pair[1], :, cols].astype(F32)
            return carry

        lax.fori_loop(0, HS // SUB, step, 0)

    def finish_images(k, carry):
        for part in range(2):
            for side in range(2):
                img_copy(side, k, part).wait_send()
        return carry

    lax.fori_loop(0, NCH, finish_images, 0)
    for copy in lse_copies:
        copy.wait_send()
    for q in range(len(plan)):
        core_copy(q).wait_send()
    for slot in range(6):
        y_copy(slot, 0 if slot < 3 else 1).wait_send()


def per_device(images, projections, noise_weight, trans_offset, search_list):
    rows, width = images.shape
    block = projections.shape[0]
    n_img = lax.axis_size("img")
    nrow = rows * NT
    any_space = pl.BlockSpec(memory_space=pl.ANY)
    smem = pl.BlockSpec(memory_space=pltpu.SMEM)
    vmem = pl.BlockSpec(memory_space=pltpu.VMEM)
    dma = pltpu.SemaphoreType.DMA
    weighted_sum, log_norm = pl.pallas_call(
        kernel,
        out_shape=(
            jax.ShapeDtypeStruct((block, width // n_img), F32),
            jax.ShapeDtypeStruct((1, rows), F32),
        ),
        in_specs=[any_space, any_space, any_space, any_space, smem, smem],
        out_specs=(vmem, vmem),
        scratch_shapes=[
            pltpu.VMEM((3 * nrow, width), BF16),
            pltpu.VMEM((2, rows, width), BF16),
            pltpu.VMEM((rows, width), BF16),
            pltpu.VMEM((block, width), BF16),
            pltpu.VMEM((N_OFF, 2, NT, HALF), F32),
            pltpu.VMEM((1, width), F32),
            pltpu.VMEM((3 * nrow, block), F32),
            pltpu.VMEM((block, 128), F32),
            pltpu.VMEM((8, 128), F32),
            pltpu.VMEM((4, 8, 128), F32),
            pltpu.VMEM((block, 3 * nrow), BF16),
            pltpu.VMEM((8, block, HS), BF16),
            pltpu.VMEM((8, block, HS), BF16),
            pltpu.VMEM((6, block, HS), BF16),
            pltpu.VMEM((6, block, HS), BF16),
            pltpu.VMEM((2, 16, PIECE), F32),
            dma((2, 2, NCH)), dma((2, 2, NCH)),
            dma((2,)), dma((NCH,)), dma((2, NCH)),
            dma((4,)), dma((4,)),
            dma((8,)), dma((8,)),
            dma((6,)), dma((6,)),
        ],
        compiler_params=pltpu.CompilerParams(
            collective_id=0, has_side_effects=True, vmem_limit_bytes=60 * 1024 * 1024
        ),
    )(images, projections, jnp.asarray(phase_tables()), noise_weight.reshape(1, width), trans_offset, search_list.T)
    return weighted_sum, log_norm.reshape(rows)


def solution(mesh):
    in_specs = (P(("img", "orient"), None), P("orient", None), P(), P("img"), P("img", None))
    out_specs = (P("orient", "img"), P(("img", "orient")))
    return jax.shard_map(
        per_device, mesh=mesh, in_specs=in_specs, out_specs=out_specs, check_vma=False
    )
```

```python
import functools
import math

import jax
import jax.numpy as jnp
import numpy as np
from jax import lax
from jax.experimental import pallas as pl
from jax.experimental.pallas import tpu as pltpu
from jax.sharding import PartitionSpec as P

BOX = 128
HALF = BOX * BOX // 2
NT = 8
N_OFF = 16
MESH = pl.DeviceIdType.MESH
FLOOR = -1e30

QUAD = HALF // 4
CHUNK = 1024
PIECE = 512
SLICE = 2048
FAR = ((0, 512), (512, 512))
NEAR = ((0, 512), (512, 512))
WINDOW = 2
F32 = jnp.float32
BF16 = jnp.bfloat16


def phase_tables():
    steps = np.arange(BOX)
    unit = 2.0 * math.pi / BOX
    cos1, sin1 = np.cos(steps * unit), np.sin(steps * unit)
    t, s, f = np.arange(N_OFF)[:, None, None], np.arange(NT)[None, :, None], np.arange(HALF)[None, None, :]
    kx, ky = f // (BOX // 2), f % (BOX // 2)
    fx = np.where(kx < BOX // 2, kx, kx - BOX)
    turn_x = (fx * (t % 4 - 2 + s % 4)) % BOX
    turn_y = (ky * (t // 4 - 2 + s // 4)) % BOX
    cx, sx, cy, sy = cos1[turn_x], sin1[turn_x], cos1[turn_y], sin1[turn_y]
    return np.stack([cx * cy - sx * sy, sx * cy + cx * sy], axis=1).astype(np.float32)


def kernel(
    img_hbm, proj_hbm, tab_hbm, w_hbm, off_hbm, list_hbm,
    sum_hbm, last_hbm, norm_hbm,
    al, other, halo, own, mate_img, wp, tab, w, off, mate_off, listed, score, mate_score, power, lse, others, post,
    ysend, yrecv, mine, norm, stage,
    img_send, img_recv, loc_sem, proj_sem, mate_send, mate_recv, small_send, small_recv,
    lse_send, lse_recv, y_send, y_recv, out_sem,
):
    rows = img_hbm.shape[0]
    nrow = rows * NT
    n_img, n_or = lax.axis_size("img"), lax.axis_size("orient")
    i, o = lax.axis_index("img"), lax.axis_index("orient")
    core = lax.rem(i, 2)
    chip = lax.div(i, 2)
    n_y = n_img // 2
    before, after = lax.rem(o + n_or - 1, n_or), lax.rem(o + 1, n_or)
    before2, after2 = lax.rem(o + n_or - 2, n_or), lax.rem(o + 2, n_or)
    mate_i = i + 1 - 2 * core
    mate = (mate_i, o)
    up = (lax.rem(i + 2, n_img), o)
    down = (lax.rem(i + n_img - 2, n_img), o)

    barrier = pltpu.get_barrier_semaphore()
    rings = [(side, place) for side in (i, mate_i) for place in (after2, before2, after, before)]
    partners = [*rings, mate, up, down]
    for dev in partners:
        pl.semaphore_signal(barrier, inc=1, device_id=dev, device_id_type=MESH)
    pl.semaphore_wait(barrier, len(partners))

    def remote(src, dst, ssem, rsem, dev):
        return pltpu.make_async_remote_copy(
            src_ref=src, dst_ref=dst, send_sem=ssem, recv_sem=rsem, device_id=dev, device_id_type=MESH
        )

    def span(start, size):
        return pl.ds(pl.multiple_of(start, PIECE), size)

    def mine_at(b):
        return (2 * b + core) * QUAD

    def theirs_at(b):
        return (2 * b + 1 - core) * QUAD

    per_quad = QUAD // CHUNK

    def img_copy(side, k, part, start, size):
        cols = span(part * HALF + start, size)
        dev = (i, after) if side == 0 else (i, before)
        return remote(
            img_hbm.at[:, cols], halo.at[side, :, cols], img_send.at[side, part, k], img_recv.at[side, part, k], dev
        )

    def theirs_copy(side, b, part):
        return img_copy(side, b, part, theirs_at(b), QUAD)

    def mine_copy(side, m, part):
        b, c = lax.div(m, per_quad), lax.rem(m, per_quad)
        return img_copy(side, 2 + m, part, mine_at(b) + c * CHUNK, CHUNK)

    ways2 = [(part, side) for part in range(2) for side in range(2)]

    def each_copy(act):
        def theirs(b, carry):
            for part, side in ways2:
                act(theirs_copy(side, b, part))
            return carry

        def mines(m, carry):
            for part, side in ways2:
                act(mine_copy(side, m, part))
            return carry

        lax.fori_loop(0, 2, theirs, 0)
        lax.fori_loop(0, 2 * per_quad, mines, 0)

    each_copy(lambda copy: copy.start())

    small = [
        pltpu.make_async_copy(off_hbm, off, loc_sem.at[3]),
        pltpu.make_async_copy(list_hbm, listed, loc_sem.at[4]),
        pltpu.make_async_copy(img_hbm, own, loc_sem.at[0]),
        pltpu.make_async_copy(w_hbm, w, loc_sem.at[1]),
    ]
    for copy in small:
        copy.start()
    off_copy = remote(off_hbm, mate_off, small_send.at[0], small_recv.at[0], mate)
    off_copy.start()

    def quad_at(q):
        return theirs_at(q) if q < 2 else mine_at(q - 2)

    def proj_copy(q, part):
        cols = span(part * HALF + quad_at(q), QUAD)
        return pltpu.make_async_copy(proj_hbm.at[:, cols], wp.at[:, cols], proj_sem.at[part, q])

    tab_copy = pltpu.make_async_copy(tab_hbm, tab, loc_sem.at[2])
    for q in range(4):
        for part in range(2):
            proj_copy(q, part).start()
        if q == 0:
            tab_copy.start()

    def to_mate(which, b, part):
        cols = span(part * HALF + theirs_at(b), QUAD)
        src = own.at[:, cols] if which == 0 else halo.at[which - 1, :, cols]
        dst = mate_img.at[which, :, span(part * 2 * QUAD + b * QUAD, QUAD)]
        return remote(src, dst, mate_send.at[which, part, b], mate_recv.at[which, part, b], mate)

    def weigh(start, size):
        def step(p, acc):
            for part in range(2):
                c = span(part * HALF + start + p * PIECE, PIECE)
                x = wp[:, c].astype(F32)
                y = x * w[:, c]
                wp[:, c] = y.astype(BF16)
                q = x * y
                for j in range(PIECE // 128):
                    acc = acc + q[:, j * 128:(j + 1) * 128]
            return acc

        power[...] += lax.fori_loop(0, size // PIECE, step, jnp.zeros(power.shape, F32))

    def align(src, src_at, offsets, block, start, size, dst, row, dst_at):
        def step(it, carry):
            g, p = lax.div(it, size // PIECE), lax.rem(it, size // PIECE)
            cols = span(start + p * PIECE, PIECE)
            r16 = pl.ds(pl.multiple_of(g * 16, 16), 16)
            for part in range(2):
                stage[part] = src[r16, span(src_at[part] + p * PIECE, PIECE)].astype(F32)
            for pair in range(8):
                res, ims = [], []
                for h in range(2):
                    n = 2 * pair + h
                    t = offsets[block * rows + g * 16 + n]
                    c = tab[t, 0, :, cols]
                    d = tab[t, 1, :, cols]
                    rb = stage[0, pl.ds(n, NT, stride=0), :]
                    ib = stage[1, pl.ds(n, NT, stride=0), :]
                    res.append(rb * c + ib * d)
                    ims.append(ib * c - rb * d)
                to = pl.ds(pl.multiple_of(row + g * 128 + pair * 16, 16), 16)
                dst[to, span(dst_at[0] + p * PIECE, PIECE)] = jnp.concatenate(res, axis=0).astype(BF16)
                dst[to, span(dst_at[1] + p * PIECE, PIECE)] = jnp.concatenate(ims, axis=0).astype(BF16)
            return carry

        lax.fori_loop(0, (rows // 16) * (size // PIECE), step, 0)

    def add_scores(src, src_rows, src_at, start, size, here):
        total = score[here, :]
        for part in range(2):
            total += lax.dot_general(
                src[src_rows, span(src_at[part], size)],
                wp[:, span(part * HALF + start, size)],
                (((1,), (1,)), ((), ())),
                preferred_element_type=F32,
            )
        score[here, :] = total

    lse[...] = jnp.zeros(lse.shape, F32)
    score[...] = jnp.zeros(score.shape, F32)
    power[...] = jnp.zeros(power.shape, F32)
    for copy in small:
        copy.wait()
    for b in range(2):
        for part in range(2):
            to_mate(0, b, part).start()
    tab_copy.wait()

    own_rows = pl.ds(0, nrow)
    halo_rows = pl.ds(nrow, 2 * nrow)
    both = pl.ds(0, 2 * nrow)
    for q in range(4):
        for part in range(2):
            proj_copy(q, part).wait()
    for q in range(4):
        start = quad_at(q)
        weigh(start, QUAD)
        dst, dst_at = (other, (0, QUAD)) if q < 2 else (al, ((q - 2) * QUAD, q * QUAD))
        align(own, (start, HALF + start), off, o, start, QUAD, dst, 0, dst_at)
        add_scores(dst, own_rows, dst_at, start, QUAD, own_rows)

    half_power = 0.5 * jnp.sum(power[...].T, axis=0, keepdims=True)
    diagonal = lax.broadcasted_iota(jnp.int32, (rows, 128), 0) == lax.broadcasted_iota(jnp.int32, (rows, 128), 1)

    def finish_scores(slot, block):
        hit = (listed[0, block] == o) | (listed[1, block] == o) | (listed[2, block] == o)
        keep = jnp.where(hit, 1.0, 0.0)
        floor = jnp.where(hit, 0.0, FLOOR)
        here = pl.ds(slot * nrow, nrow)
        x = (score[here, :] - half_power) * keep + floor
        score[here, :] = x
        x3 = x.reshape(rows, NT, 128)
        m = jnp.max(jnp.max(x3, axis=1), axis=1, keepdims=True)
        mb = jnp.broadcast_to(m, (rows, 128))
        e = jnp.exp(x3 - mb[:, None, :])
        total = jnp.sum(jnp.sum(e, axis=1), axis=1, keepdims=True)
        value = jnp.broadcast_to(m + jnp.log(total), (rows, 128))
        return jnp.sum(jnp.where(diagonal, value, 0.0), axis=0, keepdims=True)

    def score_copy(n, here):
        return remote(score.at[here], mate_score.at[here], small_send.at[1 + n], small_recv.at[1 + n], mate)

    score_copies = [score_copy(0, own_rows), score_copy(1, halo_rows)]
    lse[1:2, :] = finish_scores(0, o)
    score_copies[0].start()

    def side_block(side):
        return lax.rem(o + n_or - 1 + 2 * side, n_or)

    def mate_align(which, b):
        for part in range(2):
            to_mate(which, b, part).wait_recv()
        block = o if which == 0 else side_block(which - 1)
        at = (b * QUAD, (2 + b) * QUAD)
        align(mate_img.at[which], at, mate_off, block, mine_at(b), QUAD, al, (3 + which) * nrow, at)

    off_copy.wait_recv()
    for b in range(2):
        for part, side in ways2:
            theirs_copy(side, b, part).wait_recv()
            to_mate(1 + side, b, part).start()
        start = theirs_at(b)
        for side in range(2):
            align(halo.at[side], (start, HALF + start), off, side_block(side), start, QUAD, other, side * nrow, (0, QUAD))
        add_scores(other, both, (0, QUAD), start, QUAD, halo_rows)
        if b == 0:
            mate_align(0, 0)
            mate_align(0, 1)
        else:
            mate_align(1, 0)
            mate_align(2, 0)

    def mine_chunk(m, carry):
        for part, side in ways2:
            mine_copy(side, m, part).wait_recv()
        start = mine_at(lax.div(m, per_quad)) + lax.rem(m, per_quad) * CHUNK
        at = (m * CHUNK, 2 * QUAD + m * CHUNK)
        for side in range(2):
            align(
                halo.at[side], (start, HALF + start), off, side_block(side), start, CHUNK, al, (1 + side) * nrow, at
            )
        add_scores(al, halo_rows, at, start, CHUNK, halo_rows)
        return carry

    lax.fori_loop(0, 2 * per_quad, mine_chunk, 0)

    lse[2:3, :] = finish_scores(1, before)
    lse[0:1, :] = finish_scores(2, after)

    lse_copies = [
        remote(lse, others.at[n], lse_send.at[n], lse_recv.at[n], dev) for n, dev in enumerate([*rings, mate])
    ]
    for copy in lse_copies:
        copy.start()
    score_copies[1].start()
    mate_align(1, 1)
    mate_align(2, 1)
    for copy in lse_copies:
        copy.wait_recv()

    def combine(a, b, c):
        m = jnp.maximum(jnp.maximum(a, b), c)
        return m + jnp.log(jnp.exp(a - m) + jnp.exp(b - m) + jnp.exp(c - m))

    norms = []
    for here, n in ((lse, 0), (others.at[8], 4)):
        norms += [
            combine(here[1:2, :], others[n + 2, 0:1, :], others[n + 3, 2:3, :]),
            combine(here[2:3, :], others[n + 2, 1:2, :], others[n, 0:1, :]),
            combine(here[0:1, :], others[n + 3, 1:2, :], others[n + 1, 2:3, :]),
        ]
    norm[...] = norms[0]
    norm_copy = pltpu.make_async_copy(norm, norm_hbm, out_sem.at[4])
    norm_copy.start()

    def posterior(slot, source, at):
        x3 = source[pl.ds(at * nrow, nrow), :].reshape(rows, NT, 128)
        each = jnp.sum(jnp.where(diagonal, jnp.broadcast_to(norms[slot], (rows, 128)), 0.0), axis=1, keepdims=True)
        p = jnp.exp(x3 - jnp.broadcast_to(each, (rows, 128))[:, None, :]).reshape(nrow, 128)
        post[:, pl.ds(slot * nrow, nrow)] = p.T.astype(BF16)

    for slot in range(3):
        posterior(slot, score, slot)
    for copy in score_copies:
        copy.wait_recv()
    for slot in range(3):
        posterior(3 + slot, mate_score, slot)

    half = SLICE // 2
    chip_up, chip_down = lax.rem(chip + 1, n_y), lax.rem(chip + n_y - 1, n_y)
    chip_far = lax.rem(chip + 2, n_y)
    ways = []
    for near, base, rest in ((chip_up, 0, half), (chip_down, half, 0)):
        pieces = [(chip_far, base + at, size, None) for at, size in FAR]
        pieces += [(near, rest + at, size, None) for at, size in NEAR]
        pieces += [(near, base + at, size, n) for n, (at, size) in enumerate(FAR)]
        ways.append(pieces)
    per_way = len(ways[0])

    def sums(dest, at, size):
        return jnp.dot(
            post[...], al[:, pl.ds(pl.multiple_of(dest * SLICE + at, 128), size)], preferred_element_type=F32
        )

    def y_cols(way, n):
        return pl.ds(sum(piece[2] for piece in ways[way][:n]), ways[way][n][2])

    def y_copy(way, n):
        _, at, size, _ = ways[way][n]
        dst = yrecv.at[way, :, pl.ds(FAR[n][0], size)] if n < len(FAR) else last_hbm.at[way, :, pl.ds(at, size)]
        return remote(ysend.at[way, :, y_cols(way, n)], dst, y_send.at[way, n], y_recv.at[way, n], (up, down)[way])

    for n in range(per_way):
        for way in range(2):
            dest, at, size, add = ways[way][n]
            total = sums(dest, at, size)
            if add is not None:
                y_copy(way, add).wait_recv()
                total = total + yrecv[way, :, pl.ds(FAR[add][0], size)].astype(F32)
            ysend[way, :, y_cols(way, n)] = total.astype(BF16)
            if n >= WINDOW:
                y_copy(way, n - WINDOW).wait_send()
            y_copy(way, n).start()

    def sum_copy(n):
        cols = pl.ds(n * PIECE, PIECE)
        return pltpu.make_async_copy(mine.at[:, cols], sum_hbm.at[:, cols], out_sem.at[n])

    for n in range(SLICE // PIECE):
        mine[:, pl.ds(n * PIECE, PIECE)] = sums(chip, n * PIECE, PIECE)
        sum_copy(n).start()

    for n in range(len(FAR), per_way):
        for way in range(2):
            y_copy(way, n).wait_recv()
    each_copy(lambda copy: copy.wait_send())
    off_copy.wait_send()
    for copy in lse_copies + score_copies:
        copy.wait_send()
    for which in range(3):
        for b in range(2):
            for part in range(2):
                to_mate(which, b, part).wait_send()
    for n in range(per_way - WINDOW, per_way):
        for way in range(2):
            y_copy(way, n).wait_send()
    for n in range(SLICE // PIECE):
        sum_copy(n).wait()
    norm_copy.wait()


def finish_kernel(sum_ref, last_ref, norm_ref, out_ref, log_ref):
    out_ref[...] = sum_ref[...] + last_ref[0].astype(F32) + last_ref[1].astype(F32)
    log_ref[...] = norm_ref[:, :log_ref.shape[1]]


def per_device(images, projections, noise_weight, trans_offset, search_list):
    rows, width = images.shape
    block = projections.shape[0]
    nrow = rows * NT
    per_way = 2 * len(FAR) + len(NEAR)
    chunks = 2 + 2 * QUAD // CHUNK
    any_space = pl.BlockSpec(memory_space=pl.ANY)
    dma = pltpu.SemaphoreType.DMA
    sums, last, norms = pl.pallas_call(
        kernel,
        out_shape=(
            jax.ShapeDtypeStruct((block, SLICE), F32),
            jax.ShapeDtypeStruct((2, block, SLICE), BF16),
            jax.ShapeDtypeStruct((1, 128), F32),
        ),
        in_specs=[any_space] * 6,
        out_specs=(any_space, any_space, any_space),
        scratch_shapes=[
            pltpu.VMEM((6 * nrow, width // 2), BF16),
            pltpu.VMEM((2 * nrow, 2 * QUAD), BF16),
            pltpu.VMEM((2, rows, width), BF16),
            pltpu.VMEM((rows, width), BF16),
            pltpu.VMEM((3, rows, width // 2), BF16),
            pltpu.VMEM((block, width), BF16),
            pltpu.VMEM((N_OFF, 2, NT, HALF), F32),
            pltpu.VMEM((1, width), F32),
            pltpu.SMEM(trans_offset.shape, jnp.int32),
            pltpu.SMEM(trans_offset.shape, jnp.int32),
            pltpu.SMEM(search_list.shape[::-1], jnp.int32),
            pltpu.VMEM((3 * nrow, block), F32),
            pltpu.VMEM((3 * nrow, block), F32),
            pltpu.VMEM((block, 128), F32),
            pltpu.VMEM((8, 128), F32),
            pltpu.VMEM((9, 8, 128), F32),
            pltpu.VMEM((block, 6 * nrow), BF16),
            pltpu.VMEM((2, block, 3 * SLICE // 2), BF16),
            pltpu.VMEM((2, block, SLICE // 2), BF16),
            pltpu.VMEM((block, SLICE), F32),
            pltpu.VMEM((1, 128), F32),
            pltpu.VMEM((2, 16, PIECE), F32),
            dma((2, 2, chunks)), dma((2, 2, chunks)),
            dma((5,)), dma((2, 4)),
            dma((3, 2, 2)), dma((3, 2, 2)),
            dma((3,)), dma((3,)),
            dma((9,)), dma((9,)),
            dma((2, per_way)), dma((2, per_way)),
            dma((5,)),
        ],
        compiler_params=pltpu.CompilerParams(
            collective_id=0, has_side_effects=True, vmem_limit_bytes=60 * 1024 * 1024
        ),
    )(images, projections, jnp.asarray(phase_tables()), noise_weight.reshape(1, width), trans_offset, search_list.T)
    weighted_sum, log_norm = pl.pallas_call(
        finish_kernel,
        out_shape=(
            jax.ShapeDtypeStruct((block, SLICE), F32),
            jax.ShapeDtypeStruct((1, rows), F32),
        ),
    )(sums, last, norms)
    return weighted_sum, log_norm.reshape(rows)


def solution(mesh):
    in_specs = (P(("img", "orient"), None), P("orient", None), P(), P("img"), P("img", None))
    out_specs = (P("orient", "img"), P(("img", "orient")))
    return jax.shard_map(
        per_device, mesh=mesh, in_specs=in_specs, out_specs=out_specs, check_vma=False
    )
```

```python
import functools
import math

import jax
import jax.numpy as jnp
import numpy as np
from jax import lax
from jax.experimental import pallas as pl
from jax.experimental.pallas import tpu as pltpu
from jax.sharding import PartitionSpec as P

BOX = 128
HALF = BOX * BOX // 2
NT = 8
N_OFF = 16
MESH = pl.DeviceIdType.MESH
FLOOR = -1e30

QUAD = HALF // 4
CHUNKS = (1024, 512)
PIECE = 512
SLICE = 2048
FAR = ((0, 512), (512, 512))
NEAR = ((0, 512), (512, 512))
WINDOW = 2
F32 = jnp.float32
BF16 = jnp.bfloat16


def phase_tables():
    steps = np.arange(BOX)
    unit = 2.0 * math.pi / BOX
    cos1, sin1 = np.cos(steps * unit), np.sin(steps * unit)
    t, s, f = np.arange(N_OFF)[:, None, None], np.arange(NT)[None, :, None], np.arange(HALF)[None, None, :]
    kx, ky = f // (BOX // 2), f % (BOX // 2)
    fx = np.where(kx < BOX // 2, kx, kx - BOX)
    turn_x = (fx * (t % 4 - 2 + s % 4)) % BOX
    turn_y = (ky * (t // 4 - 2 + s // 4)) % BOX
    cx, sx, cy, sy = cos1[turn_x], sin1[turn_x], cos1[turn_y], sin1[turn_y]
    return np.stack([cx * cy - sx * sy, sx * cy + cx * sy], axis=1).astype(np.float32)


def kernel(
    img_hbm, proj_hbm, tab_hbm, w_hbm, off_hbm, list_hbm,
    sum_hbm, last_hbm, norm_hbm,
    al, other, halo, own, mate_img, wp, tab0, tab1, tab_mine, w, off, mate_off, listed, score, mate_score, power, lse, others, post,
    ysend, yrecv, mine, norm, stage,
    img_send, img_recv, loc_sem, tab_sem, proj_sem, mate_send, mate_recv, small_send, small_recv,
    lse_send, lse_recv, y_send, y_recv, out_sem,
):
    rows = img_hbm.shape[0]
    nrow = rows * NT
    n_img, n_or = lax.axis_size("img"), lax.axis_size("orient")
    i, o = lax.axis_index("img"), lax.axis_index("orient")
    core = lax.rem(i, 2)
    chip = lax.div(i, 2)
    n_y = n_img // 2
    before, after = lax.rem(o + n_or - 1, n_or), lax.rem(o + 1, n_or)
    before2, after2 = lax.rem(o + n_or - 2, n_or), lax.rem(o + 2, n_or)
    mate_i = i + 1 - 2 * core
    mate = (mate_i, o)
    up = (lax.rem(i + 2, n_img), o)
    down = (lax.rem(i + n_img - 2, n_img), o)

    barrier = pltpu.get_barrier_semaphore()
    rings = [(side, place) for side in (i, mate_i) for place in (after2, before2, after, before)]
    partners = [*rings, mate, up, down]
    for dev in partners:
        pl.semaphore_signal(barrier, inc=1, device_id=dev, device_id_type=MESH)
    pl.semaphore_wait(barrier, len(partners))

    def remote(src, dst, ssem, rsem, dev):
        return pltpu.make_async_remote_copy(
            src_ref=src, dst_ref=dst, send_sem=ssem, recv_sem=rsem, device_id=dev, device_id_type=MESH
        )

    def span(start, size):
        return pl.ds(pl.multiple_of(start, PIECE), size)

    def mine_at(b):
        return (2 * b + core) * QUAD

    def theirs_at(b):
        return (2 * b + 1 - core) * QUAD

    tabs = (tab0, tab1, tab_mine.at[0], tab_mine.at[1])
    counts = [QUAD // size for size in CHUNKS]

    def img_copy(side, k, part, start, size):
        cols = span(part * HALF + start, size)
        dev = (i, after) if side == 0 else (i, before)
        return remote(
            img_hbm.at[:, cols], halo.at[side, :, cols], img_send.at[side, part, k], img_recv.at[side, part, k], dev
        )

    def theirs_copy(side, b, part):
        return img_copy(side, b, part, theirs_at(b), QUAD)

    def mine_copy(side, b, m, part):
        return img_copy(side, 2 + b * counts[0] + m, part, mine_at(b) + m * CHUNKS[b], CHUNKS[b])

    ways2 = [(part, side) for part in range(2) for side in range(2)]

    def each_copy(act):
        def theirs(b, carry):
            for part, side in ways2:
                act(theirs_copy(side, b, part))
            return carry

        lax.fori_loop(0, 2, theirs, 0)
        for b in range(2):

            def mines(m, carry):
                for part, side in ways2:
                    act(mine_copy(side, b, m, part))
                return carry

            lax.fori_loop(0, counts[b], mines, 0)

    each_copy(lambda copy: copy.start())

    small = [
        pltpu.make_async_copy(off_hbm, off, loc_sem.at[3]),
        pltpu.make_async_copy(list_hbm, listed, loc_sem.at[4]),
        pltpu.make_async_copy(img_hbm, own, loc_sem.at[0]),
        pltpu.make_async_copy(w_hbm, w, loc_sem.at[1]),
    ]
    for copy in small:
        copy.start()
    off_copy = remote(off_hbm, mate_off, small_send.at[0], small_recv.at[0], mate)
    off_copy.start()

    def quad_at(q):
        return theirs_at(q) if q < 2 else mine_at(q - 2)

    def proj_copy(q, part):
        cols = span(part * HALF + quad_at(q), QUAD)
        return pltpu.make_async_copy(proj_hbm.at[:, cols], wp.at[:, cols], proj_sem.at[part, q])

    def tab_copy(q):
        return pltpu.make_async_copy(tab_hbm.at[:, :, :, span(quad_at(q), QUAD)], tabs[q], tab_sem.at[q])

    for q in range(4):
        tab_copy(q).start()
        for part in range(2):
            proj_copy(q, part).start()

    def to_mate(which, b, part):
        cols = span(part * HALF + theirs_at(b), QUAD)
        src = own.at[:, cols] if which == 0 else halo.at[which - 1, :, cols]
        dst = mate_img.at[which, :, span(part * 2 * QUAD + b * QUAD, QUAD)]
        return remote(src, dst, mate_send.at[which, part, b], mate_recv.at[which, part, b], mate)

    def weigh(start, size):
        def step(p, acc):
            for part in range(2):
                c = span(part * HALF + start + p * PIECE, PIECE)
                x = wp[:, c].astype(F32)
                y = x * w[:, c]
                wp[:, c] = y.astype(BF16)
                q = x * y
                for j in range(PIECE // 128):
                    acc = acc + q[:, j * 128:(j + 1) * 128]
            return acc

        power[...] += lax.fori_loop(0, size // PIECE, step, jnp.zeros(power.shape, F32))

    def align(src, src_at, offsets, block, tab, start, size, dst, row, dst_at):
        def step(it, carry):
            g, p = lax.div(it, size // PIECE), lax.rem(it, size // PIECE)
            cols = span(start + p * PIECE, PIECE)
            r16 = pl.ds(pl.multiple_of(g * 16, 16), 16)
            for part in range(2):
                stage[part] = src[r16, span(src_at[part] + p * PIECE, PIECE)].astype(F32)
            for pair in range(8):
                res, ims = [], []
                for h in range(2):
                    n = 2 * pair + h
                    t = offsets[block * rows + g * 16 + n]
                    c = tab[t, 0, :, cols]
                    d = tab[t, 1, :, cols]
                    rb = stage[0, pl.ds(n, NT, stride=0), :]
                    ib = stage[1, pl.ds(n, NT, stride=0), :]
                    res.append(rb * c + ib * d)
                    ims.append(ib * c - rb * d)
                to = pl.ds(pl.multiple_of(row + g * 128 + pair * 16, 16), 16)
                dst[to, span(dst_at[0] + p * PIECE, PIECE)] = jnp.concatenate(res, axis=0).astype(BF16)
                dst[to, span(dst_at[1] + p * PIECE, PIECE)] = jnp.concatenate(ims, axis=0).astype(BF16)
            return carry

        lax.fori_loop(0, (rows // 16) * (size // PIECE), step, 0)

    def add_scores(src, src_rows, src_at, start, size, here):
        total = score[here, :]
        for part in range(2):
            total += lax.dot_general(
                src[src_rows, span(src_at[part], size)],
                wp[:, span(part * HALF + start, size)],
                (((1,), (1,)), ((), ())),
                preferred_element_type=F32,
            )
        score[here, :] = total

    lse[...] = jnp.zeros(lse.shape, F32)
    score[...] = jnp.zeros(score.shape, F32)
    power[...] = jnp.zeros(power.shape, F32)
    for copy in small:
        copy.wait()
    for b in range(2):
        for part in range(2):
            to_mate(0, b, part).start()

    own_rows = pl.ds(0, nrow)
    halo_rows = pl.ds(nrow, 2 * nrow)
    both = pl.ds(0, 2 * nrow)
    for q in range(4):
        for part in range(2):
            proj_copy(q, part).wait()
        for table in ((0,), (1,), (2, 3), ())[q]:
            tab_copy(table).wait()
        start = quad_at(q)
        weigh(start, QUAD)
        dst, dst_at = (other, (0, QUAD)) if q < 2 else (al, ((q - 2) * QUAD, q * QUAD))
        align(own, (start, HALF + start), off, o, tabs[q], 0, QUAD, dst, 0, dst_at)
        add_scores(dst, own_rows, dst_at, start, QUAD, own_rows)

    half_power = 0.5 * jnp.sum(power[...].T, axis=0, keepdims=True)
    diagonal = lax.broadcasted_iota(jnp.int32, (rows, 128), 0) == lax.broadcasted_iota(jnp.int32, (rows, 128), 1)

    def finish_scores(slot, block):
        hit = (listed[0, block] == o) | (listed[1, block] == o) | (listed[2, block] == o)
        keep = jnp.where(hit, 1.0, 0.0)
        floor = jnp.where(hit, 0.0, FLOOR)
        here = pl.ds(slot * nrow, nrow)
        x = (score[here, :] - half_power) * keep + floor
        score[here, :] = x
        x3 = x.reshape(rows, NT, 128)
        m = jnp.max(jnp.max(x3, axis=1), axis=1, keepdims=True)
        mb = jnp.broadcast_to(m, (rows, 128))
        e = jnp.exp(x3 - mb[:, None, :])
        total = jnp.sum(jnp.sum(e, axis=1), axis=1, keepdims=True)
        value = jnp.broadcast_to(m + jnp.log(total), (rows, 128))
        return jnp.sum(jnp.where(diagonal, value, 0.0), axis=0, keepdims=True)

    def score_copy(n, here):
        return remote(score.at[here], mate_score.at[here], small_send.at[1 + n], small_recv.at[1 + n], mate)

    score_copies = [score_copy(0, own_rows), score_copy(1, halo_rows)]
    lse[1:2, :] = finish_scores(0, o)
    score_copies[0].start()

    def side_block(side):
        return lax.rem(o + n_or - 1 + 2 * side, n_or)

    def mate_align(which, b):
        for part in range(2):
            to_mate(which, b, part).wait_recv()
        block = o if which == 0 else side_block(which - 1)
        at = (b * QUAD, (2 + b) * QUAD)
        align(mate_img.at[which], at, mate_off, block, tab_mine.at[b], 0, QUAD, al, (3 + which) * nrow, at)

    far_block = lax.rem(chip, 2)
    near_block = 1 - far_block
    off_copy.wait_recv()
    for b in range(2):
        for part, side in ways2:
            theirs_copy(side, b, part).wait_recv()
            to_mate(1 + side, b, part).start()
        start = theirs_at(b)
        for side in range(2):
            align(
                halo.at[side], (start, HALF + start), off, side_block(side), tabs[b], 0, QUAD, other, side * nrow, (0, QUAD)
            )
        add_scores(other, both, (0, QUAD), start, QUAD, halo_rows)
        if b == 0:
            mate_align(0, far_block)

    for b in range(2):

        def mine_chunk(m, carry):
            for part, side in ways2:
                mine_copy(side, b, m, part).wait_recv()
            first = m * CHUNKS[b]
            start = mine_at(b) + first
            at = (b * QUAD + first, (2 + b) * QUAD + first)
            for side in range(2):
                align(
                    halo.at[side], (start, HALF + start), off, side_block(side), tabs[2 + b], first, CHUNKS[b],
                    al, (1 + side) * nrow, at,
                )
            add_scores(al, halo_rows, at, start, CHUNKS[b], halo_rows)
            return carry

        lax.fori_loop(0, counts[b], mine_chunk, 0)

    lse[2:3, :] = finish_scores(1, before)
    lse[0:1, :] = finish_scores(2, after)

    lse_copies = [
        remote(lse, others.at[n], lse_send.at[n], lse_recv.at[n], dev) for n, dev in enumerate([*rings, mate])
    ]
    for copy in lse_copies:
        copy.start()
    score_copies[1].start()
    mate_align(1, far_block)
    mate_align(2, far_block)
    for copy in lse_copies:
        copy.wait_recv()

    def combine(a, b, c):
        m = jnp.maximum(jnp.maximum(a, b), c)
        return m + jnp.log(jnp.exp(a - m) + jnp.exp(b - m) + jnp.exp(c - m))

    norms = []
    for here, n in ((lse, 0), (others.at[8], 4)):
        norms += [
            combine(here[1:2, :], others[n + 2, 0:1, :], others[n + 3, 2:3, :]),
            combine(here[2:3, :], others[n + 2, 1:2, :], others[n, 0:1, :]),
            combine(here[0:1, :], others[n + 3, 1:2, :], others[n + 1, 2:3, :]),
        ]
    norm[...] = norms[0]
    norm_copy = pltpu.make_async_copy(norm, norm_hbm, out_sem.at[4])
    norm_copy.start()

    def posterior(slot, source, at):
        x3 = source[pl.ds(at * nrow, nrow), :].reshape(rows, NT, 128)
        each = jnp.sum(jnp.where(diagonal, jnp.broadcast_to(norms[slot], (rows, 128)), 0.0), axis=1, keepdims=True)
        p = jnp.exp(x3 - jnp.broadcast_to(each, (rows, 128))[:, None, :]).reshape(nrow, 128)
        post[:, pl.ds(slot * nrow, nrow)] = p.T.astype(BF16)

    for slot in range(3):
        posterior(slot, score, slot)
    for copy in score_copies:
        copy.wait_recv()
    for slot in range(3):
        posterior(3 + slot, mate_score, slot)

    half = SLICE // 2
    chip_up, chip_down = lax.rem(chip + 1, n_y), lax.rem(chip + n_y - 1, n_y)
    chip_far = lax.rem(chip + 2, n_y)
    ways = []
    for near, base, rest in ((chip_up, 0, half), (chip_down, half, 0)):
        pieces = [(chip_far, base + at, size, None) for at, size in FAR]
        pieces += [(near, rest + at, size, None) for at, size in NEAR]
        pieces += [(near, base + at, size, n) for n, (at, size) in enumerate(FAR)]
        ways.append(pieces)
    per_way = len(ways[0])

    def sums(dest, at, size):
        return jnp.dot(
            post[...], al[:, pl.ds(pl.multiple_of(dest * SLICE + at, 128), size)], preferred_element_type=F32
        )

    def y_cols(way, n):
        return pl.ds(sum(piece[2] for piece in ways[way][:n]), ways[way][n][2])

    def y_copy(way, n):
        _, at, size, _ = ways[way][n]
        dst = yrecv.at[way, :, pl.ds(FAR[n][0], size)] if n < len(FAR) else last_hbm.at[way, :, pl.ds(at, size)]
        return remote(ysend.at[way, :, y_cols(way, n)], dst, y_send.at[way, n], y_recv.at[way, n], (up, down)[way])

    for n in range(per_way):
        if n == len(FAR):
            for which in range(3):
                mate_align(which, near_block)
        for way in range(2):
            dest, at, size, add = ways[way][n]
            total = sums(dest, at, size)
            if add is not None:
                y_copy(way, add).wait_recv()
                total = total + yrecv[way, :, pl.ds(FAR[add][0], size)].astype(F32)
            ysend[way, :, y_cols(way, n)] = total.astype(BF16)
            if n >= WINDOW:
                y_copy(way, n - WINDOW).wait_send()
            y_copy(way, n).start()

    def sum_copy(n):
        cols = pl.ds(n * PIECE, PIECE)
        return pltpu.make_async_copy(mine.at[:, cols], sum_hbm.at[:, cols], out_sem.at[n])

    for n in range(SLICE // PIECE):
        mine[:, pl.ds(n * PIECE, PIECE)] = sums(chip, n * PIECE, PIECE)
        sum_copy(n).start()

    for n in range(len(FAR), per_way):
        for way in range(2):
            y_copy(way, n).wait_recv()
    each_copy(lambda copy: copy.wait_send())
    off_copy.wait_send()
    for copy in lse_copies + score_copies:
        copy.wait_send()
    for which in range(3):
        for b in range(2):
            for part in range(2):
                to_mate(which, b, part).wait_send()
    for n in range(per_way - WINDOW, per_way):
        for way in range(2):
            y_copy(way, n).wait_send()
    for n in range(SLICE // PIECE):
        sum_copy(n).wait()
    norm_copy.wait()


def finish_kernel(sum_ref, last_ref, norm_ref, out_ref, log_ref):
    out_ref[...] = sum_ref[...] + last_ref[0].astype(F32) + last_ref[1].astype(F32)
    log_ref[...] = norm_ref[:, :log_ref.shape[1]]


def per_device(images, projections, noise_weight, trans_offset, search_list):
    rows, width = images.shape
    block = projections.shape[0]
    nrow = rows * NT
    per_way = 2 * len(FAR) + len(NEAR)
    chunks = 2 + sum(QUAD // size for size in CHUNKS)
    any_space = pl.BlockSpec(memory_space=pl.ANY)
    dma = pltpu.SemaphoreType.DMA
    sums, last, norms = pl.pallas_call(
        kernel,
        out_shape=(
            jax.ShapeDtypeStruct((block, SLICE), F32),
            jax.ShapeDtypeStruct((2, block, SLICE), BF16),
            jax.ShapeDtypeStruct((1, 128), F32),
        ),
        in_specs=[any_space] * 6,
        out_specs=(any_space, any_space, any_space),
        scratch_shapes=[
            pltpu.VMEM((6 * nrow, width // 2), BF16),
            pltpu.VMEM((2 * nrow, 2 * QUAD), BF16),
            pltpu.VMEM((2, rows, width), BF16),
            pltpu.VMEM((rows, width), BF16),
            pltpu.VMEM((3, rows, width // 2), BF16),
            pltpu.VMEM((block, width), BF16),
            pltpu.VMEM((N_OFF, 2, NT, QUAD), F32),
            pltpu.VMEM((N_OFF, 2, NT, QUAD), F32),
            pltpu.VMEM((2, N_OFF, 2, NT, QUAD), F32),
            pltpu.VMEM((1, width), F32),
            pltpu.SMEM(trans_offset.shape, jnp.int32),
            pltpu.SMEM(trans_offset.shape, jnp.int32),
            pltpu.SMEM(search_list.shape[::-1], jnp.int32),
            pltpu.VMEM((3 * nrow, block), F32),
            pltpu.VMEM((3 * nrow, block), F32),
            pltpu.VMEM((block, 128), F32),
            pltpu.VMEM((8, 128), F32),
            pltpu.VMEM((9, 8, 128), F32),
            pltpu.VMEM((block, 6 * nrow), BF16),
            pltpu.VMEM((2, block, 3 * SLICE // 2), BF16),
            pltpu.VMEM((2, block, SLICE // 2), BF16),
            pltpu.VMEM((block, SLICE), F32),
            pltpu.VMEM((1, 128), F32),
            pltpu.VMEM((2, 16, PIECE), F32),
            dma((2, 2, chunks)), dma((2, 2, chunks)),
            dma((5,)), dma((4,)), dma((2, 4)),
            dma((3, 2, 2)), dma((3, 2, 2)),
            dma((3,)), dma((3,)),
            dma((9,)), dma((9,)),
            dma((2, per_way)), dma((2, per_way)),
            dma((5,)),
        ],
        compiler_params=pltpu.CompilerParams(
            collective_id=0, has_side_effects=True, vmem_limit_bytes=60 * 1024 * 1024
        ),
    )(images, projections, jnp.asarray(phase_tables()), noise_weight.reshape(1, width), trans_offset, search_list.T)
    weighted_sum, log_norm = pl.pallas_call(
        finish_kernel,
        out_shape=(
            jax.ShapeDtypeStruct((block, SLICE), F32),
            jax.ShapeDtypeStruct((1, rows), F32),
        ),
    )(sums, last, norms)
    return weighted_sum, log_norm.reshape(rows)


def solution(mesh):
    in_specs = (P(("img", "orient"), None), P("orient", None), P(), P("img"), P("img", None))
    out_specs = (P("orient", "img"), P(("img", "orient")))
    return jax.shard_map(
        per_device, mesh=mesh, in_specs=in_specs, out_specs=out_specs, check_vma=False
    )
```

```python
import functools
import math

import jax
import jax.numpy as jnp
import numpy as np
from jax import lax
from jax.experimental import pallas as pl
from jax.experimental.pallas import tpu as pltpu
from jax.sharding import PartitionSpec as P

BOX = 128
HALF = BOX * BOX // 2
NT = 8
N_OFF = 16
MESH = pl.DeviceIdType.MESH
FLOOR = -1e30

QUAD = HALF // 4
CHUNKS = (1024, 512)
PIECE = 512
SLICE = 2048
FAR = ((0, 512), (512, 512))
NEAR = ((0, 512), (512, 512))
WINDOW = 2
F32 = jnp.float32
BF16 = jnp.bfloat16


def phase_tables():
    steps = np.arange(BOX)
    unit = 2.0 * math.pi / BOX
    cos1, sin1 = np.cos(steps * unit), np.sin(steps * unit)
    t, s, f = np.arange(N_OFF)[:, None, None], np.arange(NT)[None, :, None], np.arange(HALF)[None, None, :]
    kx, ky = f // (BOX // 2), f % (BOX // 2)
    fx = np.where(kx < BOX // 2, kx, kx - BOX)
    turn_x = (fx * (t % 4 - 2 + s % 4)) % BOX
    turn_y = (ky * (t // 4 - 2 + s // 4)) % BOX
    cx, sx, cy, sy = cos1[turn_x], sin1[turn_x], cos1[turn_y], sin1[turn_y]
    return np.stack([cx * cy - sx * sy, sx * cy + cx * sy], axis=1).astype(np.float32)


def kernel(
    img_hbm, proj_hbm, tab_hbm, w_hbm, off_hbm, list_hbm,
    sum_hbm, last_hbm, norm_hbm,
    al, other, halo, own, mate_img, wp, tab0, tab1, tab_mine, w, off, mate_off, listed, score, mate_score, power, lse, others, turned, post,
    ysend, yrecv, mine, norm, stage,
    img_send, img_recv, loc_sem, tab_sem, proj_sem, mate_send, mate_recv, small_send, small_recv,
    lse_send, lse_recv, y_send, y_recv, out_sem,
):
    rows = img_hbm.shape[0]
    nrow = rows * NT
    n_img, n_or = lax.axis_size("img"), lax.axis_size("orient")
    i, o = lax.axis_index("img"), lax.axis_index("orient")
    core = lax.rem(i, 2)
    chip = lax.div(i, 2)
    n_y = n_img // 2
    before, after = lax.rem(o + n_or - 1, n_or), lax.rem(o + 1, n_or)
    before2, after2 = lax.rem(o + n_or - 2, n_or), lax.rem(o + 2, n_or)
    mate_i = i + 1 - 2 * core
    mate = (mate_i, o)
    up = (lax.rem(i + 2, n_img), o)
    down = (lax.rem(i + n_img - 2, n_img), o)

    barrier = pltpu.get_barrier_semaphore()
    rings = [(side, place) for side in (i, mate_i) for place in (after2, before2, after, before)]
    partners = [*rings[2:4], *rings[:2], *rings[4:], mate, up, down]
    for dev in partners:
        pl.semaphore_signal(barrier, inc=1, device_id=dev, device_id_type=MESH)
    pl.semaphore_wait(barrier, len(partners))

    def remote(src, dst, ssem, rsem, dev):
        return pltpu.make_async_remote_copy(
            src_ref=src, dst_ref=dst, send_sem=ssem, recv_sem=rsem, device_id=dev, device_id_type=MESH
        )

    def span(start, size):
        return pl.ds(pl.multiple_of(start, PIECE), size)

    def mine_at(b):
        return (2 * b + core) * QUAD

    def theirs_at(b):
        return (2 * b + 1 - core) * QUAD

    tabs = (tab0, tab1, tab_mine.at[0], tab_mine.at[1])
    counts = [QUAD // size for size in CHUNKS]

    def img_copy(side, k, part, start, size):
        cols = span(part * HALF + start, size)
        dev = (i, after) if side == 0 else (i, before)
        return remote(
            img_hbm.at[:, cols], halo.at[side, :, cols], img_send.at[side, part, k], img_recv.at[side, part, k], dev
        )

    def theirs_copy(side, b, part):
        return img_copy(side, b, part, theirs_at(b), QUAD)

    def mine_copy(side, b, m, part):
        return img_copy(side, 2 + b * counts[0] + m, part, mine_at(b) + m * CHUNKS[b], CHUNKS[b])

    ways2 = [(part, side) for part in range(2) for side in range(2)]

    def each_copy(act):
        def theirs(b, carry):
            for part, side in ways2:
                act(theirs_copy(side, b, part))
            return carry

        lax.fori_loop(0, 2, theirs, 0)
        for b in range(2):

            def mines(m, carry):
                for part, side in ways2:
                    act(mine_copy(side, b, m, part))
                return carry

            lax.fori_loop(0, counts[b], mines, 0)

    each_copy(lambda copy: copy.start())

    small = [
        pltpu.make_async_copy(off_hbm, off, loc_sem.at[3]),
        pltpu.make_async_copy(list_hbm, listed, loc_sem.at[4]),
        pltpu.make_async_copy(img_hbm, own, loc_sem.at[0]),
        pltpu.make_async_copy(w_hbm, w, loc_sem.at[1]),
    ]
    for copy in small:
        copy.start()
    off_copy = remote(off_hbm, mate_off, small_send.at[0], small_recv.at[0], mate)
    off_copy.start()

    def quad_at(q):
        return theirs_at(q) if q < 2 else mine_at(q - 2)

    def proj_copy(q, part):
        cols = span(part * HALF + quad_at(q), QUAD)
        return pltpu.make_async_copy(proj_hbm.at[:, cols], wp.at[:, cols], proj_sem.at[part, q])

    def tab_copy(q):
        return pltpu.make_async_copy(tab_hbm.at[:, :, :, span(quad_at(q), QUAD)], tabs[q], tab_sem.at[q])

    for q in range(4):
        tab_copy(q).start()
        for part in range(2):
            proj_copy(q, part).start()

    def to_mate(which, b, part):
        cols = span(part * HALF + theirs_at(b), QUAD)
        src = own.at[:, cols] if which == 0 else halo.at[which - 1, :, cols]
        dst = mate_img.at[which, :, span(part * 2 * QUAD + b * QUAD, QUAD)]
        return remote(src, dst, mate_send.at[which, part, b], mate_recv.at[which, part, b], mate)

    def weigh(start, size):
        def step(p, acc):
            for part in range(2):
                c = span(part * HALF + start + p * PIECE, PIECE)
                x = wp[:, c].astype(F32)
                y = x * w[:, c]
                wp[:, c] = y.astype(BF16)
                q = x * y
                for j in range(PIECE // 128):
                    acc = acc + q[:, j * 128:(j + 1) * 128]
            return acc

        power[...] += lax.fori_loop(0, size // PIECE, step, jnp.zeros(power.shape, F32))

    def align(src, src_at, offsets, block, tab, start, size, dst, row, dst_at):
        def step(it, carry):
            g, p = lax.div(it, size // PIECE), lax.rem(it, size // PIECE)
            cols = span(start + p * PIECE, PIECE)
            r16 = pl.ds(pl.multiple_of(g * 16, 16), 16)
            for part in range(2):
                stage[part] = src[r16, span(src_at[part] + p * PIECE, PIECE)].astype(F32)
            for pair in range(8):
                res, ims = [], []
                for h in range(2):
                    n = 2 * pair + h
                    t = offsets[block * rows + g * 16 + n]
                    c = tab[t, 0, :, cols]
                    d = tab[t, 1, :, cols]
                    rb = stage[0, pl.ds(n, NT, stride=0), :]
                    ib = stage[1, pl.ds(n, NT, stride=0), :]
                    res.append(rb * c + ib * d)
                    ims.append(ib * c - rb * d)
                to = pl.ds(pl.multiple_of(row + g * 128 + pair * 16, 16), 16)
                dst[to, span(dst_at[0] + p * PIECE, PIECE)] = jnp.concatenate(res, axis=0).astype(BF16)
                dst[to, span(dst_at[1] + p * PIECE, PIECE)] = jnp.concatenate(ims, axis=0).astype(BF16)
            return carry

        lax.fori_loop(0, (rows // 16) * (size // PIECE), step, 0)

    def add_scores(src, src_rows, src_at, start, size, here):
        total = score[here, :]
        for part in range(2):
            total += lax.dot_general(
                src[src_rows, span(src_at[part], size)],
                wp[:, span(part * HALF + start, size)],
                (((1,), (1,)), ((), ())),
                preferred_element_type=F32,
            )
        score[here, :] = total

    lse[...] = jnp.zeros(lse.shape, F32)
    score[...] = jnp.zeros(score.shape, F32)
    power[...] = jnp.zeros(power.shape, F32)
    for copy in small:
        copy.wait()
    for b in range(2):
        for part in range(2):
            to_mate(0, b, part).start()

    own_rows = pl.ds(0, nrow)
    halo_rows = pl.ds(nrow, 2 * nrow)
    both = pl.ds(0, 2 * nrow)
    for q in range(4):
        for part in range(2):
            proj_copy(q, part).wait()
        for table in ((0,), (1,), (2, 3), ())[q]:
            tab_copy(table).wait()
        start = quad_at(q)
        weigh(start, QUAD)
        dst, dst_at = (other, (0, QUAD)) if q < 2 else (al, ((q - 2) * QUAD, q * QUAD))
        align(own, (start, HALF + start), off, o, tabs[q], 0, QUAD, dst, 0, dst_at)
        add_scores(dst, own_rows, dst_at, start, QUAD, own_rows)

    half_power = 0.5 * jnp.sum(power[...].T, axis=0, keepdims=True)
    diagonal = lax.broadcasted_iota(jnp.int32, (rows, 128), 0) == lax.broadcasted_iota(jnp.int32, (rows, 128), 1)

    def finish_scores(slot, block):
        hit = (listed[0, block] == o) | (listed[1, block] == o) | (listed[2, block] == o)
        keep = jnp.where(hit, 1.0, 0.0)
        floor = jnp.where(hit, 0.0, FLOOR)
        here = pl.ds(slot * nrow, nrow)
        x = (score[here, :] - half_power) * keep + floor
        score[here, :] = x
        x3 = x.reshape(rows, NT, 128)
        m = jnp.max(jnp.max(x3, axis=1), axis=1, keepdims=True)
        mb = jnp.broadcast_to(m, (rows, 128))
        e = jnp.exp(x3 - mb[:, None, :])
        total = jnp.sum(jnp.sum(e, axis=1), axis=1, keepdims=True)
        value = jnp.broadcast_to(m + jnp.log(total), (rows, 128))
        return jnp.sum(jnp.where(diagonal, value, 0.0), axis=0, keepdims=True)

    def score_copy(n, here):
        return remote(score.at[here], mate_score.at[here], small_send.at[1 + n], small_recv.at[1 + n], mate)

    score_copies = [score_copy(0, own_rows), score_copy(1, halo_rows)]
    lse[1:2, :] = finish_scores(0, o)
    score_copies[0].start()

    def side_block(side):
        return lax.rem(o + n_or - 1 + 2 * side, n_or)

    def mate_align(which, b):
        for part in range(2):
            to_mate(which, b, part).wait_recv()
        block = o if which == 0 else side_block(which - 1)
        at = (b * QUAD, (2 + b) * QUAD)
        align(mate_img.at[which], at, mate_off, block, tab_mine.at[b], 0, QUAD, al, (3 + which) * nrow, at)

    far_block = lax.rem(chip, 2)
    near_block = 1 - far_block
    off_copy.wait_recv()
    for b in range(2):
        for part, side in ways2:
            theirs_copy(side, b, part).wait_recv()
            to_mate(1 + side, b, part).start()
        start = theirs_at(b)
        for side in range(2):
            align(
                halo.at[side], (start, HALF + start), off, side_block(side), tabs[b], 0, QUAD, other, side * nrow, (0, QUAD)
            )
        add_scores(other, both, (0, QUAD), start, QUAD, halo_rows)
        if b == 0:
            mate_align(0, far_block)

    for b in range(2):

        def mine_chunk(m, carry):
            for part, side in ways2:
                mine_copy(side, b, m, part).wait_recv()
            first = m * CHUNKS[b]
            start = mine_at(b) + first
            at = (b * QUAD + first, (2 + b) * QUAD + first)
            for side in range(2):
                align(
                    halo.at[side], (start, HALF + start), off, side_block(side), tabs[2 + b], first, CHUNKS[b],
                    al, (1 + side) * nrow, at,
                )
            add_scores(al, halo_rows, at, start, CHUNKS[b], halo_rows)
            return carry

        lax.fori_loop(0, counts[b], mine_chunk, 0)

    lse[2:3, :] = finish_scores(1, before)
    lse[0:1, :] = finish_scores(2, after)

    lse_copies = [
        remote(lse, others.at[n], lse_send.at[n], lse_recv.at[n], dev) for n, dev in enumerate([*rings, mate])
    ]
    for copy in lse_copies:
        copy.start()
    score_copies[1].start()

    def turn(slot, source, at):
        turned[:, pl.ds(slot * nrow, nrow)] = source[pl.ds(at * nrow, nrow), :].T

    for slot in range(3):
        turn(slot, score, slot)
    score_copies[0].wait_recv()
    turn(3, mate_score, 0)
    mate_align(1, far_block)
    mate_align(2, far_block)
    for copy in lse_copies:
        copy.wait_recv()

    def combine(a, b, c):
        m = jnp.maximum(jnp.maximum(a, b), c)
        return m + jnp.log(jnp.exp(a - m) + jnp.exp(b - m) + jnp.exp(c - m))

    norms = []
    for here, n in ((lse, 0), (others.at[8], 4)):
        norms += [
            combine(here[1:2, :], others[n + 2, 0:1, :], others[n + 3, 2:3, :]),
            combine(here[2:3, :], others[n + 2, 1:2, :], others[n, 0:1, :]),
            combine(here[0:1, :], others[n + 3, 1:2, :], others[n + 1, 2:3, :]),
        ]
    norm[...] = norms[0]
    norm_copy = pltpu.make_async_copy(norm, norm_hbm, out_sem.at[4])
    norm_copy.start()

    place = lax.broadcasted_iota(jnp.int32, (rows, nrow), 1) - NT * lax.broadcasted_iota(jnp.int32, (rows, nrow), 0)
    own_lanes = (place >= 0) & (place < NT)

    def posterior(slot):
        each = jnp.sum(jnp.where(diagonal, jnp.broadcast_to(norms[slot], (rows, 128)), 0.0), axis=1, keepdims=True)
        wide = jnp.sum(jnp.where(own_lanes, jnp.broadcast_to(each, (rows, nrow)), 0.0), axis=0, keepdims=True)
        here = pl.ds(slot * nrow, nrow)
        post[:, here] = jnp.exp(turned[:, here] - wide).astype(BF16)

    for slot in range(4):
        posterior(slot)
    score_copies[1].wait_recv()
    for slot in range(4, 6):
        turn(slot, mate_score, slot - 3)
        posterior(slot)

    half = SLICE // 2
    chip_up, chip_down = lax.rem(chip + 1, n_y), lax.rem(chip + n_y - 1, n_y)
    chip_far = lax.rem(chip + 2, n_y)
    ways = []
    for near, base, rest in ((chip_up, 0, half), (chip_down, half, 0)):
        pieces = [(chip_far, base + at, size, None) for at, size in FAR]
        pieces += [(near, rest + at, size, None) for at, size in NEAR]
        pieces += [(near, base + at, size, n) for n, (at, size) in enumerate(FAR)]
        ways.append(pieces)
    per_way = len(ways[0])

    def sums(dest, at, size):
        return jnp.dot(
            post[...], al[:, pl.ds(pl.multiple_of(dest * SLICE + at, 128), size)], preferred_element_type=F32
        )

    def y_cols(way, n):
        return pl.ds(sum(piece[2] for piece in ways[way][:n]), ways[way][n][2])

    def y_copy(way, n):
        _, at, size, _ = ways[way][n]
        dst = yrecv.at[way, :, pl.ds(FAR[n][0], size)] if n < len(FAR) else last_hbm.at[way, :, pl.ds(at, size)]
        return remote(ysend.at[way, :, y_cols(way, n)], dst, y_send.at[way, n], y_recv.at[way, n], (up, down)[way])

    for n in range(per_way):
        if n == len(FAR):
            for which in range(3):
                mate_align(which, near_block)
        for way in range(2):
            dest, at, size, add = ways[way][n]
            total = sums(dest, at, size)
            if add is not None:
                y_copy(way, add).wait_recv()
                total = total + yrecv[way, :, pl.ds(FAR[add][0], size)].astype(F32)
            ysend[way, :, y_cols(way, n)] = total.astype(BF16)
            if n >= WINDOW:
                y_copy(way, n - WINDOW).wait_send()
            y_copy(way, n).start()

    def sum_copy(n):
        cols = pl.ds(n * PIECE, PIECE)
        return pltpu.make_async_copy(mine.at[:, cols], sum_hbm.at[:, cols], out_sem.at[n])

    for n in range(SLICE // PIECE):
        mine[:, pl.ds(n * PIECE, PIECE)] = sums(chip, n * PIECE, PIECE)
        sum_copy(n).start()

    for n in range(len(FAR), per_way):
        for way in range(2):
            y_copy(way, n).wait_recv()
    each_copy(lambda copy: copy.wait_send())
    off_copy.wait_send()
    for copy in lse_copies + score_copies:
        copy.wait_send()
    for which in range(3):
        for b in range(2):
            for part in range(2):
                to_mate(which, b, part).wait_send()
    for n in range(per_way - WINDOW, per_way):
        for way in range(2):
            y_copy(way, n).wait_send()
    for n in range(SLICE // PIECE):
        sum_copy(n).wait()
    norm_copy.wait()


def finish_kernel(sum_ref, last_ref, norm_ref, out_ref, log_ref):
    out_ref[...] = sum_ref[...] + last_ref[0].astype(F32) + last_ref[1].astype(F32)
    log_ref[...] = norm_ref[:, :log_ref.shape[1]]


def per_device(images, projections, noise_weight, trans_offset, search_list):
    rows, width = images.shape
    block = projections.shape[0]
    nrow = rows * NT
    per_way = 2 * len(FAR) + len(NEAR)
    chunks = 2 + sum(QUAD // size for size in CHUNKS)
    any_space = pl.BlockSpec(memory_space=pl.ANY)
    dma = pltpu.SemaphoreType.DMA
    sums, last, norms = pl.pallas_call(
        kernel,
        out_shape=(
            jax.ShapeDtypeStruct((block, SLICE), F32),
            jax.ShapeDtypeStruct((2, block, SLICE), BF16),
            jax.ShapeDtypeStruct((1, 128), F32),
        ),
        in_specs=[any_space] * 6,
        out_specs=(any_space, any_space, any_space),
        scratch_shapes=[
            pltpu.VMEM((6 * nrow, width // 2), BF16),
            pltpu.VMEM((2 * nrow, 2 * QUAD), BF16),
            pltpu.VMEM((2, rows, width), BF16),
            pltpu.VMEM((rows, width), BF16),
            pltpu.VMEM((3, rows, width // 2), BF16),
            pltpu.VMEM((block, width), BF16),
            pltpu.VMEM((N_OFF, 2, NT, QUAD), F32),
            pltpu.VMEM((N_OFF, 2, NT, QUAD), F32),
            pltpu.VMEM((2, N_OFF, 2, NT, QUAD), F32),
            pltpu.VMEM((1, width), F32),
            pltpu.SMEM(trans_offset.shape, jnp.int32),
            pltpu.SMEM(trans_offset.shape, jnp.int32),
            pltpu.SMEM(search_list.shape[::-1], jnp.int32),
            pltpu.VMEM((3 * nrow, block), F32),
            pltpu.VMEM((3 * nrow, block), F32),
            pltpu.VMEM((block, 128), F32),
            pltpu.VMEM((8, 128), F32),
            pltpu.VMEM((9, 8, 128), F32),
            pltpu.VMEM((block, 6 * nrow), F32),
            pltpu.VMEM((block, 6 * nrow), BF16),
            pltpu.VMEM((2, block, 3 * SLICE // 2), BF16),
            pltpu.VMEM((2, block, SLICE // 2), BF16),
            pltpu.VMEM((block, SLICE), F32),
            pltpu.VMEM((1, 128), F32),
            pltpu.VMEM((2, 16, PIECE), F32),
            dma((2, 2, chunks)), dma((2, 2, chunks)),
            dma((5,)), dma((4,)), dma((2, 4)),
            dma((3, 2, 2)), dma((3, 2, 2)),
            dma((3,)), dma((3,)),
            dma((9,)), dma((9,)),
            dma((2, per_way)), dma((2, per_way)),
            dma((5,)),
        ],
        compiler_params=pltpu.CompilerParams(
            collective_id=0, has_side_effects=True, vmem_limit_bytes=60 * 1024 * 1024
        ),
    )(images, projections, jnp.asarray(phase_tables()), noise_weight.reshape(1, width), trans_offset, search_list.T)
    weighted_sum, log_norm = pl.pallas_call(
        finish_kernel,
        out_shape=(
            jax.ShapeDtypeStruct((block, SLICE), F32),
            jax.ShapeDtypeStruct((1, rows), F32),
        ),
    )(sums, last, norms)
    return weighted_sum, log_norm.reshape(rows)


def solution(mesh):
    in_specs = (P(("img", "orient"), None), P("orient", None), P(), P("img"), P("img", None))
    out_specs = (P("orient", "img"), P(("img", "orient")))
    return jax.shard_map(
        per_device, mesh=mesh, in_specs=in_specs, out_specs=out_specs, check_vma=False
    )
```

```python
import functools
import math

import jax
import jax.numpy as jnp
import numpy as np
from jax import lax
from jax.experimental import pallas as pl
from jax.experimental.pallas import tpu as pltpu
from jax.sharding import PartitionSpec as P

BOX = 128
HALF = BOX * BOX // 2
NT = 8
N_OFF = 16
MESH = pl.DeviceIdType.MESH
FLOOR = -1e30

QUAD = HALF // 4
CHUNKS = (1024, 512)
PIECE = 512
SLICE = 2048
FAR = ((0, 512), (512, 512))
NEAR = ((0, 512), (512, 512))
WINDOW = 2
F32 = jnp.float32
BF16 = jnp.bfloat16


def phase_tables():
    steps = np.arange(BOX)
    unit = 2.0 * math.pi / BOX
    cos1, sin1 = np.cos(steps * unit), np.sin(steps * unit)
    t, s, f = np.arange(N_OFF)[:, None, None], np.arange(NT)[None, :, None], np.arange(HALF)[None, None, :]
    kx, ky = f // (BOX // 2), f % (BOX // 2)
    fx = np.where(kx < BOX // 2, kx, kx - BOX)
    turn_x = (fx * (t % 4 - 2 + s % 4)) % BOX
    turn_y = (ky * (t // 4 - 2 + s // 4)) % BOX
    cx, sx, cy, sy = cos1[turn_x], sin1[turn_x], cos1[turn_y], sin1[turn_y]
    return np.stack([cx * cy - sx * sy, sx * cy + cx * sy], axis=1).astype(np.float32)


def kernel(
    img_hbm, proj_hbm, tab_hbm, w_hbm, off_hbm, list_hbm,
    sum_hbm, last_hbm, norm_hbm,
    al, other, halo, own, mate_img, wp, tab0, tab1, tab_mine, w, off, mate_off, listed, score, mate_score, power, lse, others, turned, post,
    ysend, yrecv, mine, norm, stage,
    img_send, img_recv, loc_sem, tab_sem, proj_sem, mate_send, mate_recv, small_send, small_recv,
    lse_send, lse_recv, y_send, y_recv, out_sem,
):
    rows = img_hbm.shape[0]
    nrow = rows * NT
    n_img, n_or = lax.axis_size("img"), lax.axis_size("orient")
    i, o = lax.axis_index("img"), lax.axis_index("orient")
    core = lax.rem(i, 2)
    chip = lax.div(i, 2)
    n_y = n_img // 2
    before, after = lax.rem(o + n_or - 1, n_or), lax.rem(o + 1, n_or)
    before2, after2 = lax.rem(o + n_or - 2, n_or), lax.rem(o + 2, n_or)
    mate_i = i + 1 - 2 * core
    mate = (mate_i, o)
    up = (lax.rem(i + 2, n_img), o)
    down = (lax.rem(i + n_img - 2, n_img), o)

    barrier = pltpu.get_barrier_semaphore()
    rings = [(side, place) for side in (i, mate_i) for place in (after2, before2, after, before)]
    partners = [*rings[2:4], *rings[:2], *rings[4:], mate, up, down]
    for dev in partners:
        pl.semaphore_signal(barrier, inc=1, device_id=dev, device_id_type=MESH)
    pl.semaphore_wait(barrier, len(partners))

    def remote(src, dst, ssem, rsem, dev):
        return pltpu.make_async_remote_copy(
            src_ref=src, dst_ref=dst, send_sem=ssem, recv_sem=rsem, device_id=dev, device_id_type=MESH
        )

    def span(start, size):
        return pl.ds(pl.multiple_of(start, PIECE), size)

    def mine_at(b):
        return (2 * b + core) * QUAD

    def theirs_at(b):
        return (2 * b + 1 - core) * QUAD

    tabs = (tab0, tab1, tab_mine.at[0], tab_mine.at[1])
    counts = [QUAD // size for size in CHUNKS]

    def img_copy(side, k, part, start, size):
        cols = span(part * HALF + start, size)
        dev = (i, after) if side == 0 else (i, before)
        return remote(
            img_hbm.at[:, cols], halo.at[side, :, cols], img_send.at[side, part, k], img_recv.at[side, part, k], dev
        )

    def theirs_copy(side, b, part):
        return img_copy(side, b, part, theirs_at(b), QUAD)

    def mine_copy(side, b, m, part):
        return img_copy(side, 2 + b * counts[0] + m, part, mine_at(b) + m * CHUNKS[b], CHUNKS[b])

    ways2 = [(part, side) for part in range(2) for side in range(2)]

    def each_copy(act):
        def theirs(b, carry):
            for part, side in ways2:
                act(theirs_copy(side, b, part))
            return carry

        lax.fori_loop(0, 2, theirs, 0)
        for b in range(2):

            def mines(m, carry):
                for part, side in ways2:
                    act(mine_copy(side, b, m, part))
                return carry

            lax.fori_loop(0, counts[b], mines, 0)

    each_copy(lambda copy: copy.start())

    small = [
        pltpu.make_async_copy(off_hbm, off, loc_sem.at[3]),
        pltpu.make_async_copy(list_hbm, listed, loc_sem.at[4]),
        pltpu.make_async_copy(img_hbm, own, loc_sem.at[0]),
        pltpu.make_async_copy(w_hbm, w, loc_sem.at[1]),
    ]
    for copy in small:
        copy.start()
    off_copy = remote(off_hbm, mate_off, small_send.at[0], small_recv.at[0], mate)
    off_copy.start()

    def quad_at(q):
        return theirs_at(q) if q < 2 else mine_at(q - 2)

    def proj_copy(q, part):
        cols = span(part * HALF + quad_at(q), QUAD)
        return pltpu.make_async_copy(proj_hbm.at[:, cols], wp.at[:, cols], proj_sem.at[part, q])

    def tab_copy(q):
        return pltpu.make_async_copy(tab_hbm.at[:, :, :, span(quad_at(q), QUAD)], tabs[q], tab_sem.at[q])

    for q in range(4):
        tab_copy(q).start()
        for part in range(2):
            proj_copy(q, part).start()

    def to_mate(which, b, part):
        cols = span(part * HALF + theirs_at(b), QUAD)
        src = own.at[:, cols] if which == 0 else halo.at[which - 1, :, cols]
        dst = mate_img.at[which, :, span(part * 2 * QUAD + b * QUAD, QUAD)]
        return remote(src, dst, mate_send.at[which, part, b], mate_recv.at[which, part, b], mate)

    def weigh(start, size):
        def step(p, acc):
            for part in range(2):
                c = span(part * HALF + start + p * PIECE, PIECE)
                x = wp[:, c].astype(F32)
                y = x * w[:, c]
                wp[:, c] = y.astype(BF16)
                q = x * y
                for j in range(PIECE // 128):
                    acc = acc + q[:, j * 128:(j + 1) * 128]
            return acc

        power[...] += lax.fori_loop(0, size // PIECE, step, jnp.zeros(power.shape, F32))

    def align(src, src_at, offsets, block, tab, start, size, dst, row, dst_at):
        def step(it, carry):
            g, p = lax.div(it, size // PIECE), lax.rem(it, size // PIECE)
            cols = span(start + p * PIECE, PIECE)
            r16 = pl.ds(pl.multiple_of(g * 16, 16), 16)
            for part in range(2):
                stage[part, pl.ds(0, 16), :] = src[r16, span(src_at[part] + p * PIECE, PIECE)].astype(F32)
            for pair in range(8):
                res, ims = [], []
                for h in range(2):
                    n = 2 * pair + h
                    t = offsets[block * rows + g * 16 + n]
                    c = tab[t, 0, :, cols]
                    d = tab[t, 1, :, cols]
                    rb = stage[0, pl.ds(n, NT, stride=0), :]
                    ib = stage[1, pl.ds(n, NT, stride=0), :]
                    res.append(rb * c + ib * d)
                    ims.append(ib * c - rb * d)
                to = pl.ds(pl.multiple_of(row + g * 128 + pair * 16, 16), 16)
                dst[to, span(dst_at[0] + p * PIECE, PIECE)] = jnp.concatenate(res, axis=0).astype(BF16)
                dst[to, span(dst_at[1] + p * PIECE, PIECE)] = jnp.concatenate(ims, axis=0).astype(BF16)
            return carry

        lax.fori_loop(0, (rows // 16) * (size // PIECE), step, 0)

    def add_scores(src, src_rows, src_at, start, size, here):
        total = score[here, :]
        for part in range(2):
            total += lax.dot_general(
                src[src_rows, span(src_at[part], size)],
                wp[:, span(part * HALF + start, size)],
                (((1,), (1,)), ((), ())),
                preferred_element_type=F32,
            )
        score[here, :] = total

    lse[...] = jnp.zeros(lse.shape, F32)
    score[...] = jnp.zeros(score.shape, F32)
    power[...] = jnp.zeros(power.shape, F32)
    for copy in small:
        copy.wait()
    for b in range(2):
        for part in range(2):
            to_mate(0, b, part).start()

    own_rows = pl.ds(0, nrow)
    halo_rows = pl.ds(nrow, 2 * nrow)
    both = pl.ds(0, 2 * nrow)
    for q in range(4):
        for part in range(2):
            proj_copy(q, part).wait()
        for table in ((0,), (1,), (2, 3), ())[q]:
            tab_copy(table).wait()
        start = quad_at(q)
        weigh(start, QUAD)
        dst, dst_at = (other, (0, QUAD)) if q < 2 else (al, ((q - 2) * QUAD, q * QUAD))
        align(own, (start, HALF + start), off, o, tabs[q], 0, QUAD, dst, 0, dst_at)
        add_scores(dst, own_rows, dst_at, start, QUAD, own_rows)

    half_power = 0.5 * jnp.sum(power[...].T, axis=0, keepdims=True)
    diagonal = lax.broadcasted_iota(jnp.int32, (rows, 128), 0) == lax.broadcasted_iota(jnp.int32, (rows, 128), 1)

    def finish_scores(slot, block):
        hit = (listed[0, block] == o) | (listed[1, block] == o) | (listed[2, block] == o)
        keep = jnp.where(hit, 1.0, 0.0)
        floor = jnp.where(hit, 0.0, FLOOR)
        here = pl.ds(slot * nrow, nrow)
        x = (score[here, :] - half_power) * keep + floor
        score[here, :] = x
        x3 = x.reshape(rows, NT, 128)
        m = jnp.max(jnp.max(x3, axis=1), axis=1, keepdims=True)
        mb = jnp.broadcast_to(m, (rows, 128))
        e = jnp.exp(x3 - mb[:, None, :])
        total = jnp.sum(jnp.sum(e, axis=1), axis=1, keepdims=True)
        value = jnp.broadcast_to(m + jnp.log(total), (rows, 128))
        return jnp.sum(jnp.where(diagonal, value, 0.0), axis=0, keepdims=True)

    def score_copy(n, here):
        return remote(score.at[here], mate_score.at[here], small_send.at[1 + n], small_recv.at[1 + n], mate)

    score_copies = [score_copy(0, own_rows), score_copy(1, halo_rows)]
    lse[1:2, :] = finish_scores(0, o)
    score_copies[0].start()

    def side_block(side):
        return lax.rem(o + n_or - 1 + 2 * side, n_or)

    def mate_align(which, b):
        for part in range(2):
            to_mate(which, b, part).wait_recv()
        block = o if which == 0 else side_block(which - 1)
        at = (b * QUAD, (2 + b) * QUAD)
        align(mate_img.at[which], at, mate_off, block, tab_mine.at[b], 0, QUAD, al, (3 + which) * nrow, at)

    far_block = lax.rem(chip, 2)
    near_block = 1 - far_block
    off_copy.wait_recv()
    for b in range(2):
        for part, side in ways2:
            theirs_copy(side, b, part).wait_recv()
            to_mate(1 + side, b, part).start()
        start = theirs_at(b)
        for side in range(2):
            align(
                halo.at[side], (start, HALF + start), off, side_block(side), tabs[b], 0, QUAD, other, side * nrow, (0, QUAD)
            )
        add_scores(other, both, (0, QUAD), start, QUAD, halo_rows)
        if b == 0:
            mate_align(0, far_block)

    for b in range(2):

        def mine_chunk(m, carry):
            for part, side in ways2:
                mine_copy(side, b, m, part).wait_recv()
            first = m * CHUNKS[b]
            start = mine_at(b) + first
            at = (b * QUAD + first, (2 + b) * QUAD + first)
            for side in range(2):
                align(
                    halo.at[side], (start, HALF + start), off, side_block(side), tabs[2 + b], first, CHUNKS[b],
                    al, (1 + side) * nrow, at,
                )
            add_scores(al, halo_rows, at, start, CHUNKS[b], halo_rows)
            return carry

        lax.fori_loop(0, counts[b], mine_chunk, 0)

    lse[2:3, :] = finish_scores(1, before)
    lse[0:1, :] = finish_scores(2, after)

    lse_copies = [
        remote(lse, others.at[n], lse_send.at[n], lse_recv.at[n], dev) for n, dev in enumerate([*rings, mate])
    ]
    for copy in lse_copies:
        copy.start()
    score_copies[1].start()

    def turn(slot, source, at):
        turned[:, pl.ds(slot * nrow, nrow)] = source[pl.ds(at * nrow, nrow), :].T

    for slot in range(3):
        turn(slot, score, slot)
    score_copies[0].wait_recv()
    turn(3, mate_score, 0)
    mate_align(1, far_block)
    mate_align(2, far_block)
    for copy in lse_copies:
        copy.wait_recv()

    def combine(a, b, c):
        m = jnp.maximum(jnp.maximum(a, b), c)
        return m + jnp.log(jnp.exp(a - m) + jnp.exp(b - m) + jnp.exp(c - m))

    norms = []
    for here, n in ((lse, 0), (others.at[8], 4)):
        norms += [
            combine(here[1:2, :], others[n + 2, 0:1, :], others[n + 3, 2:3, :]),
            combine(here[2:3, :], others[n + 2, 1:2, :], others[n, 0:1, :]),
            combine(here[0:1, :], others[n + 3, 1:2, :], others[n + 1, 2:3, :]),
        ]
    norm[...] = norms[0]
    norm_copy = pltpu.make_async_copy(norm, norm_hbm, out_sem.at[4])
    norm_copy.start()

    place = lax.broadcasted_iota(jnp.int32, (rows, nrow), 1) - NT * lax.broadcasted_iota(jnp.int32, (rows, nrow), 0)
    own_lanes = (place >= 0) & (place < NT)

    def posterior(slot):
        each = jnp.sum(jnp.where(diagonal, jnp.broadcast_to(norms[slot], (rows, 128)), 0.0), axis=1, keepdims=True)
        wide = jnp.sum(jnp.where(own_lanes, jnp.broadcast_to(each, (rows, nrow)), 0.0), axis=0, keepdims=True)
        here = pl.ds(slot * nrow, nrow)
        post[:, here] = jnp.exp(turned[:, here] - wide).astype(BF16)

    for slot in range(4):
        posterior(slot)
    score_copies[1].wait_recv()
    for slot in range(4, 6):
        turn(slot, mate_score, slot - 3)
        posterior(slot)

    half = SLICE // 2
    chip_up, chip_down = lax.rem(chip + 1, n_y), lax.rem(chip + n_y - 1, n_y)
    chip_far = lax.rem(chip + 2, n_y)
    ways = []
    for near, base, rest in ((chip_up, 0, half), (chip_down, half, 0)):
        pieces = [(chip_far, base + at, size, None) for at, size in FAR]
        pieces += [(near, rest + at, size, None) for at, size in NEAR]
        pieces += [(near, base + at, size, n) for n, (at, size) in enumerate(FAR)]
        ways.append(pieces)
    per_way = len(ways[0])

    def sums(dest, at, size):
        return jnp.dot(
            post[...], al[:, pl.ds(pl.multiple_of(dest * SLICE + at, 128), size)], preferred_element_type=F32
        )

    def y_cols(way, n):
        return pl.ds(sum(piece[2] for piece in ways[way][:n]), ways[way][n][2])

    def y_copy(way, n):
        _, at, size, _ = ways[way][n]
        dst = yrecv.at[way, :, pl.ds(FAR[n][0], size)] if n < len(FAR) else last_hbm.at[way, :, pl.ds(at, size)]
        return remote(ysend.at[way, :, y_cols(way, n)], dst, y_send.at[way, n], y_recv.at[way, n], (up, down)[way])

    for n in range(per_way):
        if n == len(FAR):
            for which in range(3):
                mate_align(which, near_block)
        for way in range(2):
            dest, at, size, add = ways[way][n]
            total = sums(dest, at, size)
            if add is not None:
                y_copy(way, add).wait_recv()
                total = total + yrecv[way, :, pl.ds(FAR[add][0], size)].astype(F32)
            ysend[way, :, y_cols(way, n)] = total.astype(BF16)
            if n >= WINDOW:
                y_copy(way, n - WINDOW).wait_send()
            y_copy(way, n).start()

    def sum_copy(n):
        cols = pl.ds(n * PIECE, PIECE)
        return pltpu.make_async_copy(mine.at[:, cols], sum_hbm.at[:, cols], out_sem.at[n])

    for n in range(SLICE // PIECE):
        mine[:, pl.ds(n * PIECE, PIECE)] = sums(chip, n * PIECE, PIECE)
        sum_copy(n).start()

    for n in range(len(FAR), per_way):
        for way in range(2):
            y_copy(way, n).wait_recv()
    each_copy(lambda copy: copy.wait_send())
    off_copy.wait_send()
    for copy in lse_copies + score_copies:
        copy.wait_send()
    for which in range(3):
        for b in range(2):
            for part in range(2):
                to_mate(which, b, part).wait_send()
    for n in range(per_way - WINDOW, per_way):
        for way in range(2):
            y_copy(way, n).wait_send()
    for n in range(SLICE // PIECE):
        sum_copy(n).wait()
    norm_copy.wait()


def finish_kernel(sum_ref, last_ref, norm_ref, out_ref, log_ref):
    out_ref[...] = sum_ref[...] + last_ref[0].astype(F32) + last_ref[1].astype(F32)
    log_ref[...] = norm_ref[:, :log_ref.shape[1]]


def per_device(images, projections, noise_weight, trans_offset, search_list):
    rows, width = images.shape
    block = projections.shape[0]
    nrow = rows * NT
    per_way = 2 * len(FAR) + len(NEAR)
    chunks = 2 + sum(QUAD // size for size in CHUNKS)
    any_space = pl.BlockSpec(memory_space=pl.ANY)
    dma = pltpu.SemaphoreType.DMA
    sums, last, norms = pl.pallas_call(
        kernel,
        out_shape=(
            jax.ShapeDtypeStruct((block, SLICE), F32),
            jax.ShapeDtypeStruct((2, block, SLICE), BF16),
            jax.ShapeDtypeStruct((1, 128), F32),
        ),
        in_specs=[any_space] * 6,
        out_specs=(any_space, any_space, any_space),
        scratch_shapes=[
            pltpu.VMEM((6 * nrow, width // 2), BF16),
            pltpu.VMEM((2 * nrow, 2 * QUAD), BF16),
            pltpu.VMEM((2, rows, width), BF16),
            pltpu.VMEM((rows, width), BF16),
            pltpu.VMEM((3, rows, width // 2), BF16),
            pltpu.VMEM((block, width), BF16),
            pltpu.VMEM((N_OFF, 2, NT, QUAD), F32),
            pltpu.VMEM((N_OFF, 2, NT, QUAD), F32),
            pltpu.VMEM((2, N_OFF, 2, NT, QUAD), F32),
            pltpu.VMEM((1, width), F32),
            pltpu.SMEM(trans_offset.shape, jnp.int32),
            pltpu.SMEM(trans_offset.shape, jnp.int32),
            pltpu.SMEM(search_list.shape[::-1], jnp.int32),
            pltpu.VMEM((3 * nrow, block), F32),
            pltpu.VMEM((3 * nrow, block), F32),
            pltpu.VMEM((block, 128), F32),
            pltpu.VMEM((8, 128), F32),
            pltpu.VMEM((9, 8, 128), F32),
            pltpu.VMEM((block, 6 * nrow), F32),
            pltpu.VMEM((block, 6 * nrow), BF16),
            pltpu.VMEM((2, block, 3 * SLICE // 2), BF16),
            pltpu.VMEM((2, block, SLICE // 2), BF16),
            pltpu.VMEM((block, SLICE), F32),
            pltpu.VMEM((1, 128), F32),
            pltpu.VMEM((2, 24, PIECE), F32),
            dma((2, 2, chunks)), dma((2, 2, chunks)),
            dma((5,)), dma((4,)), dma((2, 4)),
            dma((3, 2, 2)), dma((3, 2, 2)),
            dma((3,)), dma((3,)),
            dma((9,)), dma((9,)),
            dma((2, per_way)), dma((2, per_way)),
            dma((5,)),
        ],
        compiler_params=pltpu.CompilerParams(
            collective_id=0, has_side_effects=True, vmem_limit_bytes=60 * 1024 * 1024
        ),
    )(images, projections, jnp.asarray(phase_tables()), noise_weight.reshape(1, width), trans_offset, search_list.T)
    weighted_sum, log_norm = pl.pallas_call(
        finish_kernel,
        out_shape=(
            jax.ShapeDtypeStruct((block, SLICE), F32),
            jax.ShapeDtypeStruct((1, rows), F32),
        ),
    )(sums, last, norms)
    return weighted_sum, log_norm.reshape(rows)


def solution(mesh):
    in_specs = (P(("img", "orient"), None), P("orient", None), P(), P("img"), P("img", None))
    out_specs = (P("orient", "img"), P(("img", "orient")))
    return jax.shard_map(
        per_device, mesh=mesh, in_specs=in_specs, out_specs=out_specs, check_vma=False
    )
```

```python
import functools
import math

import jax
import jax.numpy as jnp
import numpy as np
from jax import lax
from jax.experimental import pallas as pl
from jax.experimental.pallas import tpu as pltpu
from jax.sharding import PartitionSpec as P

BOX = 128
HALF = BOX * BOX // 2
NT = 8
N_OFF = 16
MESH = pl.DeviceIdType.MESH
FLOOR = -1e30

QUAD = HALF // 4
CHUNKS = (1024, 512)
PIECE = 512
SLICE = 2048
FAR = ((0, 1024),)
NEAR = ((0, 1024),)
WINDOW = 1
F32 = jnp.float32
BF16 = jnp.bfloat16


def phase_tables():
    steps = np.arange(BOX)
    unit = 2.0 * math.pi / BOX
    cos1, sin1 = np.cos(steps * unit), np.sin(steps * unit)
    t, s, f = np.arange(N_OFF)[:, None, None], np.arange(NT)[None, :, None], np.arange(HALF)[None, None, :]
    kx, ky = f // (BOX // 2), f % (BOX // 2)
    fx = np.where(kx < BOX // 2, kx, kx - BOX)
    turn_x = (fx * (t % 4 - 2 + s % 4)) % BOX
    turn_y = (ky * (t // 4 - 2 + s // 4)) % BOX
    cx, sx, cy, sy = cos1[turn_x], sin1[turn_x], cos1[turn_y], sin1[turn_y]
    return np.stack([cx * cy - sx * sy, sx * cy + cx * sy], axis=1).astype(np.float32)


def kernel(
    img_hbm, proj_hbm, tab_hbm, w_hbm, off_hbm, list_hbm,
    sum_hbm, last_hbm, norm_hbm,
    al, other, halo, own, mate_img, wp, tab0, tab1, tab_mine, w, off, mate_off, listed, score, mate_score, power, lse, others, turned, post,
    ysend, yrecv, mine, norm, stage,
    img_send, img_recv, loc_sem, tab_sem, proj_sem, mate_send, mate_recv, small_send, small_recv,
    lse_send, lse_recv, y_send, y_recv, out_sem,
):
    rows = img_hbm.shape[0]
    nrow = rows * NT
    n_img, n_or = lax.axis_size("img"), lax.axis_size("orient")
    i, o = lax.axis_index("img"), lax.axis_index("orient")
    core = lax.rem(i, 2)
    chip = lax.div(i, 2)
    n_y = n_img // 2
    before, after = lax.rem(o + n_or - 1, n_or), lax.rem(o + 1, n_or)
    before2, after2 = lax.rem(o + n_or - 2, n_or), lax.rem(o + 2, n_or)
    mate_i = i + 1 - 2 * core
    mate = (mate_i, o)
    up = (lax.rem(i + 2, n_img), o)
    down = (lax.rem(i + n_img - 2, n_img), o)

    barrier = pltpu.get_barrier_semaphore()
    rings = [(side, place) for side in (i, mate_i) for place in (after2, before2, after, before)]
    partners = [*rings[2:4], *rings[:2], *rings[4:], mate, up, down]
    for dev in partners:
        pl.semaphore_signal(barrier, inc=1, device_id=dev, device_id_type=MESH)
    pl.semaphore_wait(barrier, len(partners))

    def remote(src, dst, ssem, rsem, dev):
        return pltpu.make_async_remote_copy(
            src_ref=src, dst_ref=dst, send_sem=ssem, recv_sem=rsem, device_id=dev, device_id_type=MESH
        )

    def span(start, size):
        return pl.ds(pl.multiple_of(start, PIECE), size)

    def mine_at(b):
        return (2 * b + core) * QUAD

    def theirs_at(b):
        return (2 * b + 1 - core) * QUAD

    tabs = (tab0, tab1, tab_mine.at[0], tab_mine.at[1])
    counts = [QUAD // size for size in CHUNKS]

    def img_copy(side, k, part, start, size):
        cols = span(part * HALF + start, size)
        dev = (i, after) if side == 0 else (i, before)
        return remote(
            img_hbm.at[:, cols], halo.at[side, :, cols], img_send.at[side, part, k], img_recv.at[side, part, k], dev
        )

    def theirs_copy(side, b, part):
        return img_copy(side, b, part, theirs_at(b), QUAD)

    def mine_copy(side, b, m, part):
        return img_copy(side, 2 + b * counts[0] + m, part, mine_at(b) + m * CHUNKS[b], CHUNKS[b])

    ways2 = [(part, side) for part in range(2) for side in range(2)]

    def each_copy(act):
        def theirs(b, carry):
            for part, side in ways2:
                act(theirs_copy(side, b, part))
            return carry

        lax.fori_loop(0, 2, theirs, 0)
        for b in range(2):

            def mines(m, carry):
                for part, side in ways2:
                    act(mine_copy(side, b, m, part))
                return carry

            lax.fori_loop(0, counts[b], mines, 0)

    each_copy(lambda copy: copy.start())

    small = [
        pltpu.make_async_copy(off_hbm, off, loc_sem.at[3]),
        pltpu.make_async_copy(list_hbm, listed, loc_sem.at[4]),
        pltpu.make_async_copy(img_hbm, own, loc_sem.at[0]),
        pltpu.make_async_copy(w_hbm, w, loc_sem.at[1]),
    ]
    for copy in small:
        copy.start()
    off_copy = remote(off_hbm, mate_off, small_send.at[0], small_recv.at[0], mate)
    off_copy.start()

    def quad_at(q):
        return theirs_at(q) if q < 2 else mine_at(q - 2)

    def proj_copy(q, part):
        cols = span(part * HALF + quad_at(q), QUAD)
        return pltpu.make_async_copy(proj_hbm.at[:, cols], wp.at[:, cols], proj_sem.at[part, q])

    def tab_copy(q):
        return pltpu.make_async_copy(tab_hbm.at[:, :, :, span(quad_at(q), QUAD)], tabs[q], tab_sem.at[q])

    for q in range(4):
        tab_copy(q).start()
        for part in range(2):
            proj_copy(q, part).start()

    def to_mate(which, b, part):
        cols = span(part * HALF + theirs_at(b), QUAD)
        src = own.at[:, cols] if which == 0 else halo.at[which - 1, :, cols]
        dst = mate_img.at[which, :, span(part * 2 * QUAD + b * QUAD, QUAD)]
        return remote(src, dst, mate_send.at[which, part, b], mate_recv.at[which, part, b], mate)

    def weigh(start, size):
        def step(p, acc):
            for part in range(2):
                c = span(part * HALF + start + p * PIECE, PIECE)
                x = wp[:, c].astype(F32)
                y = x * w[:, c]
                wp[:, c] = y.astype(BF16)
                q = x * y
                for j in range(PIECE // 128):
                    acc = acc + q[:, j * 128:(j + 1) * 128]
            return acc

        power[...] += lax.fori_loop(0, size // PIECE, step, jnp.zeros(power.shape, F32))

    def align(src, src_at, offsets, block, tab, start, size, dst, row, dst_at):
        def step(it, carry):
            g, p = lax.div(it, size // PIECE), lax.rem(it, size // PIECE)
            cols = span(start + p * PIECE, PIECE)
            r16 = pl.ds(pl.multiple_of(g * 16, 16), 16)
            for part in range(2):
                stage[part, pl.ds(0, 16), :] = src[r16, span(src_at[part] + p * PIECE, PIECE)].astype(F32)
            for pair in range(8):
                res, ims = [], []
                for h in range(2):
                    n = 2 * pair + h
                    t = offsets[block * rows + g * 16 + n]
                    c = tab[t, 0, :, cols]
                    d = tab[t, 1, :, cols]
                    rb = stage[0, pl.ds(n, NT, stride=0), :]
                    ib = stage[1, pl.ds(n, NT, stride=0), :]
                    res.append(rb * c + ib * d)
                    ims.append(ib * c - rb * d)
                to = pl.ds(pl.multiple_of(row + g * 128 + pair * 16, 16), 16)
                dst[to, span(dst_at[0] + p * PIECE, PIECE)] = jnp.concatenate(res, axis=0).astype(BF16)
                dst[to, span(dst_at[1] + p * PIECE, PIECE)] = jnp.concatenate(ims, axis=0).astype(BF16)
            return carry

        lax.fori_loop(0, (rows // 16) * (size // PIECE), step, 0)

    def add_scores(src, src_rows, src_at, start, size, here):
        total = score[here, :]
        for part in range(2):
            total += lax.dot_general(
                src[src_rows, span(src_at[part], size)],
                wp[:, span(part * HALF + start, size)],
                (((1,), (1,)), ((), ())),
                preferred_element_type=F32,
            )
        score[here, :] = total

    lse[...] = jnp.zeros(lse.shape, F32)
    score[...] = jnp.zeros(score.shape, F32)
    power[...] = jnp.zeros(power.shape, F32)
    for copy in small:
        copy.wait()
    for b in range(2):
        for part in range(2):
            to_mate(0, b, part).start()

    own_rows = pl.ds(0, nrow)
    halo_rows = pl.ds(nrow, 2 * nrow)
    both = pl.ds(0, 2 * nrow)
    for q in range(4):
        for part in range(2):
            proj_copy(q, part).wait()
        for table in ((0,), (1,), (2, 3), ())[q]:
            tab_copy(table).wait()
        start = quad_at(q)
        weigh(start, QUAD)
        dst, dst_at = (other, (0, QUAD)) if q < 2 else (al, ((q - 2) * QUAD, q * QUAD))
        align(own, (start, HALF + start), off, o, tabs[q], 0, QUAD, dst, 0, dst_at)
        add_scores(dst, own_rows, dst_at, start, QUAD, own_rows)

    half_power = 0.5 * jnp.sum(power[...].T, axis=0, keepdims=True)
    diagonal = lax.broadcasted_iota(jnp.int32, (rows, 128), 0) == lax.broadcasted_iota(jnp.int32, (rows, 128), 1)

    def finish_scores(slot, block):
        hit = (listed[0, block] == o) | (listed[1, block] == o) | (listed[2, block] == o)
        keep = jnp.where(hit, 1.0, 0.0)
        floor = jnp.where(hit, 0.0, FLOOR)
        here = pl.ds(slot * nrow, nrow)
        x = (score[here, :] - half_power) * keep + floor
        score[here, :] = x
        x3 = x.reshape(rows, NT, 128)
        m = jnp.max(jnp.max(x3, axis=1), axis=1, keepdims=True)
        mb = jnp.broadcast_to(m, (rows, 128))
        e = jnp.exp(x3 - mb[:, None, :])
        total = jnp.sum(jnp.sum(e, axis=1), axis=1, keepdims=True)
        value = jnp.broadcast_to(m + jnp.log(total), (rows, 128))
        return jnp.sum(jnp.where(diagonal, value, 0.0), axis=0, keepdims=True)

    def score_copy(n, here):
        return remote(score.at[here], mate_score.at[here], small_send.at[1 + n], small_recv.at[1 + n], mate)

    score_copies = [score_copy(0, own_rows), score_copy(1, halo_rows)]
    lse[1:2, :] = finish_scores(0, o)
    score_copies[0].start()

    def side_block(side):
        return lax.rem(o + n_or - 1 + 2 * side, n_or)

    def mate_align(which, b):
        for part in range(2):
            to_mate(which, b, part).wait_recv()
        block = o if which == 0 else side_block(which - 1)
        at = (b * QUAD, (2 + b) * QUAD)
        align(mate_img.at[which], at, mate_off, block, tab_mine.at[b], 0, QUAD, al, (3 + which) * nrow, at)

    far_block = lax.rem(chip, 2)
    near_block = 1 - far_block
    off_copy.wait_recv()
    for b in range(2):
        for part, side in ways2:
            theirs_copy(side, b, part).wait_recv()
            to_mate(1 + side, b, part).start()
        start = theirs_at(b)
        for side in range(2):
            align(
                halo.at[side], (start, HALF + start), off, side_block(side), tabs[b], 0, QUAD, other, side * nrow, (0, QUAD)
            )
        add_scores(other, both, (0, QUAD), start, QUAD, halo_rows)
        if b == 0:
            mate_align(0, far_block)

    for b in range(2):

        def mine_chunk(m, carry):
            for part, side in ways2:
                mine_copy(side, b, m, part).wait_recv()
            first = m * CHUNKS[b]
            start = mine_at(b) + first
            at = (b * QUAD + first, (2 + b) * QUAD + first)
            for side in range(2):
                align(
                    halo.at[side], (start, HALF + start), off, side_block(side), tabs[2 + b], first, CHUNKS[b],
                    al, (1 + side) * nrow, at,
                )
            add_scores(al, halo_rows, at, start, CHUNKS[b], halo_rows)
            return carry

        lax.fori_loop(0, counts[b], mine_chunk, 0)

    lse[2:3, :] = finish_scores(1, before)
    lse[0:1, :] = finish_scores(2, after)

    lse_copies = [
        remote(lse, others.at[n], lse_send.at[n], lse_recv.at[n], dev) for n, dev in enumerate([*rings, mate])
    ]
    for copy in lse_copies:
        copy.start()
    score_copies[1].start()

    def turn(slot, source, at):
        turned[:, pl.ds(slot * nrow, nrow)] = source[pl.ds(at * nrow, nrow), :].T

    for slot in range(3):
        turn(slot, score, slot)
    score_copies[0].wait_recv()
    turn(3, mate_score, 0)
    mate_align(1, far_block)
    mate_align(2, far_block)
    for copy in lse_copies:
        copy.wait_recv()

    def combine(a, b, c):
        m = jnp.maximum(jnp.maximum(a, b), c)
        return m + jnp.log(jnp.exp(a - m) + jnp.exp(b - m) + jnp.exp(c - m))

    norms = []
    for here, n in ((lse, 0), (others.at[8], 4)):
        norms += [
            combine(here[1:2, :], others[n + 2, 0:1, :], others[n + 3, 2:3, :]),
            combine(here[2:3, :], others[n + 2, 1:2, :], others[n, 0:1, :]),
            combine(here[0:1, :], others[n + 3, 1:2, :], others[n + 1, 2:3, :]),
        ]
    norm[...] = norms[0]
    norm_copy = pltpu.make_async_copy(norm, norm_hbm, out_sem.at[4])
    norm_copy.start()

    place = lax.broadcasted_iota(jnp.int32, (rows, nrow), 1) - NT * lax.broadcasted_iota(jnp.int32, (rows, nrow), 0)
    own_lanes = (place >= 0) & (place < NT)

    def posterior(slot):
        each = jnp.sum(jnp.where(diagonal, jnp.broadcast_to(norms[slot], (rows, 128)), 0.0), axis=1, keepdims=True)
        wide = jnp.sum(jnp.where(own_lanes, jnp.broadcast_to(each, (rows, nrow)), 0.0), axis=0, keepdims=True)
        here = pl.ds(slot * nrow, nrow)
        post[:, here] = jnp.exp(turned[:, here] - wide).astype(BF16)

    for slot in range(4):
        posterior(slot)
    score_copies[1].wait_recv()
    for slot in range(4, 6):
        turn(slot, mate_score, slot - 3)
        posterior(slot)

    half = SLICE // 2
    chip_up, chip_down = lax.rem(chip + 1, n_y), lax.rem(chip + n_y - 1, n_y)
    chip_far = lax.rem(chip + 2, n_y)
    ways = []
    for near, base, rest in ((chip_up, 0, half), (chip_down, half, 0)):
        pieces = [(chip_far, base + at, size, None) for at, size in FAR]
        pieces += [(near, rest + at, size, None) for at, size in NEAR]
        pieces += [(near, base + at, size, n) for n, (at, size) in enumerate(FAR)]
        ways.append(pieces)
    per_way = len(ways[0])

    def sums(dest, at, size):
        return jnp.dot(
            post[...], al[:, pl.ds(pl.multiple_of(dest * SLICE + at, 128), size)], preferred_element_type=F32
        )

    def y_cols(way, n):
        return pl.ds(sum(piece[2] for piece in ways[way][:n]), ways[way][n][2])

    def y_copy(way, n):
        _, at, size, _ = ways[way][n]
        dst = yrecv.at[way, :, pl.ds(FAR[n][0], size)] if n < len(FAR) else last_hbm.at[way, :, pl.ds(at, size)]
        return remote(ysend.at[way, :, y_cols(way, n)], dst, y_send.at[way, n], y_recv.at[way, n], (up, down)[way])

    for n in range(per_way):
        if n == len(FAR):
            for which in range(3):
                mate_align(which, near_block)
        for way in range(2):
            dest, at, size, add = ways[way][n]
            total = sums(dest, at, size)
            if add is not None:
                y_copy(way, add).wait_recv()
                total = total + yrecv[way, :, pl.ds(FAR[add][0], size)].astype(F32)
            ysend[way, :, y_cols(way, n)] = total.astype(BF16)
            if n >= WINDOW:
                y_copy(way, n - WINDOW).wait_send()
            y_copy(way, n).start()

    def sum_copy(n):
        cols = pl.ds(n * PIECE, PIECE)
        return pltpu.make_async_copy(mine.at[:, cols], sum_hbm.at[:, cols], out_sem.at[n])

    for n in range(SLICE // PIECE):
        mine[:, pl.ds(n * PIECE, PIECE)] = sums(chip, n * PIECE, PIECE)
        sum_copy(n).start()

    for n in range(len(FAR), per_way):
        for way in range(2):
            y_copy(way, n).wait_recv()
    each_copy(lambda copy: copy.wait_send())
    off_copy.wait_send()
    for copy in lse_copies + score_copies:
        copy.wait_send()
    for which in range(3):
        for b in range(2):
            for part in range(2):
                to_mate(which, b, part).wait_send()
    for n in range(per_way - WINDOW, per_way):
        for way in range(2):
            y_copy(way, n).wait_send()
    for n in range(SLICE // PIECE):
        sum_copy(n).wait()
    norm_copy.wait()


def finish_kernel(sum_ref, last_ref, norm_ref, out_ref, log_ref):
    out_ref[...] = sum_ref[...] + last_ref[0].astype(F32) + last_ref[1].astype(F32)
    log_ref[...] = norm_ref[:, :log_ref.shape[1]]


def per_device(images, projections, noise_weight, trans_offset, search_list):
    rows, width = images.shape
    block = projections.shape[0]
    nrow = rows * NT
    per_way = 2 * len(FAR) + len(NEAR)
    chunks = 2 + sum(QUAD // size for size in CHUNKS)
    any_space = pl.BlockSpec(memory_space=pl.ANY)
    dma = pltpu.SemaphoreType.DMA
    sums, last, norms = pl.pallas_call(
        kernel,
        out_shape=(
            jax.ShapeDtypeStruct((block, SLICE), F32),
            jax.ShapeDtypeStruct((2, block, SLICE), BF16),
            jax.ShapeDtypeStruct((1, 128), F32),
        ),
        in_specs=[any_space] * 6,
        out_specs=(any_space, any_space, any_space),
        scratch_shapes=[
            pltpu.VMEM((6 * nrow, width // 2), BF16),
            pltpu.VMEM((2 * nrow, 2 * QUAD), BF16),
            pltpu.VMEM((2, rows, width), BF16),
            pltpu.VMEM((rows, width), BF16),
            pltpu.VMEM((3, rows, width // 2), BF16),
            pltpu.VMEM((block, width), BF16),
            pltpu.VMEM((N_OFF, 2, NT, QUAD), F32),
            pltpu.VMEM((N_OFF, 2, NT, QUAD), F32),
            pltpu.VMEM((2, N_OFF, 2, NT, QUAD), F32),
            pltpu.VMEM((1, width), F32),
            pltpu.SMEM(trans_offset.shape, jnp.int32),
            pltpu.SMEM(trans_offset.shape, jnp.int32),
            pltpu.SMEM(search_list.shape[::-1], jnp.int32),
            pltpu.VMEM((3 * nrow, block), F32),
            pltpu.VMEM((3 * nrow, block), F32),
            pltpu.VMEM((block, 128), F32),
            pltpu.VMEM((8, 128), F32),
            pltpu.VMEM((9, 8, 128), F32),
            pltpu.VMEM((block, 6 * nrow), F32),
            pltpu.VMEM((block, 6 * nrow), BF16),
            pltpu.VMEM((2, block, 3 * SLICE // 2), BF16),
            pltpu.VMEM((2, block, SLICE // 2), BF16),
            pltpu.VMEM((block, SLICE), F32),
            pltpu.VMEM((1, 128), F32),
            pltpu.VMEM((2, 24, PIECE), F32),
            dma((2, 2, chunks)), dma((2, 2, chunks)),
            dma((5,)), dma((4,)), dma((2, 4)),
            dma((3, 2, 2)), dma((3, 2, 2)),
            dma((3,)), dma((3,)),
            dma((9,)), dma((9,)),
            dma((2, per_way)), dma((2, per_way)),
            dma((5,)),
        ],
        compiler_params=pltpu.CompilerParams(
            collective_id=0, has_side_effects=True, vmem_limit_bytes=60 * 1024 * 1024
        ),
    )(images, projections, jnp.asarray(phase_tables()), noise_weight.reshape(1, width), trans_offset, search_list.T)
    weighted_sum, log_norm = pl.pallas_call(
        finish_kernel,
        out_shape=(
            jax.ShapeDtypeStruct((block, SLICE), F32),
            jax.ShapeDtypeStruct((1, rows), F32),
        ),
    )(sums, last, norms)
    return weighted_sum, log_norm.reshape(rows)


def solution(mesh):
    in_specs = (P(("img", "orient"), None), P("orient", None), P(), P("img"), P("img", None))
    out_specs = (P("orient", "img"), P(("img", "orient")))
    return jax.shard_map(
        per_device, mesh=mesh, in_specs=in_specs, out_specs=out_specs, check_vma=False
    )
```
